32 devices in a mesh: stn: 8 (over z, core), seg: 4 (over y, x).
Axes of the slice: x: 2, y: 2, z: 4, core: 2. Of those that a mesh axis runs over, the one named last changes fastest.
Arguments:
- voltages: bfloat16 [128, 32, 8192], P('stn', None, 'seg'), may hold values from -91 to 91
- filter_taps: float32 [8, 32], replicated, may hold values from -0.375 to 0.375
- positions: float32 [2, 128], replicated, may hold values from -8 to 8
- beam_dirs: int32 [128], replicated, may hold values from 0 to 359
- chan_table: int32 [16], replicated, may hold values from 0 to 15, each once
Outputs:
- beam_out: bfloat16 [16, 2, 128, 8192], P('stn', None, None, 'seg')
The draws below stay inside these ranges and needn't reach their ends.
All inputs are finite; a program needn't handle non-finite values.
Results may differ from the reference program's by a relative error of at most 0.0078.
Values may be sent and summed in bfloat16 or wider, within the bound.
No kernel may reach another device: no remote copies, remote signals or barrier semaphores. Data moves between devices by JAX's collectives and lax.ppermute only.
A program may use at most 64 MiB of HBM per device.

```python
import math
import jax
import jax.numpy as jnp
from jax import lax

S = 128
C = 16
TAPS = 8
B = 128
DIRS = 360
INTERF = 8
DMAX = 64
SNAPS = 8192
N_STN = 8


def draw_voltages(key, part):
    keys = jax.random.split(jax.random.fold_in(key, 7), 6)
    samples = SNAPS * 2 * C
    noise_part = 0.1 * jax.random.truncated_normal(keys[0], -4.0, 4.0, (S, samples), jnp.float32)
    amplitudes = jax.random.uniform(keys[3], (INTERF,), jnp.float32, 0.5, 2.0)
    station_gain = jnp.exp(jax.random.uniform(keys[5], (S, 1), jnp.float32, math.log(0.7), math.log(1.4)))
    sources = jax.random.truncated_normal(keys[1], -4.0, 4.0, (INTERF, samples + DMAX), jnp.float32)
    delays = jax.random.randint(keys[2], (INTERF, S), 0, DMAX)

    def add_source(index, summed):
        source_row = sources[index]
        shifted = jax.vmap(lambda offset: lax.dynamic_slice_in_dim(source_row, offset, samples))(delays[index])
        return summed + amplitudes[index] * shifted
    summed = lax.fori_loop(0, INTERF, add_source, noise_part) * station_gain
    return summed.reshape(S, SNAPS, 2 * C).transpose(0, 2, 1).astype(jnp.bfloat16)


def plant(drawn, rng, low, largest):
    index_at = [jax.random.randint(jax.random.fold_in(rng, axis), (), 0, length) for axis, length in enumerate(drawn.shape)]
    widest = drawn.shape.index(max(drawn.shape))
    beside = index_at[:widest] + [(index_at[widest] + 1) % drawn.shape[widest]] + index_at[widest + 1:]
    return drawn.at[tuple(index_at)].set(low).at[tuple(beside)].set(largest)


def normal_values(key, shape, width, bound, kind=jnp.bfloat16):
    return jnp.clip(width * jax.random.normal(key, shape, jnp.float32), -bound, bound).astype(kind)


def setup_inputs(seed: int = 0) -> dict:
    key_of = jax.random.split(jax.random.key(seed), 6)
    return {
        "voltages": draw_voltages(jax.random.fold_in(key_of[5], 71), 0),
        "filter_taps": normal_values(key_of[1], (TAPS, 2 * C), (TAPS * 2 * C) ** -0.5, 0.375, jnp.float32),
        "positions": jnp.clip(jax.random.uniform(key_of[2], (2, S), jnp.float32, -8.0, 8.0), -8.0, 8.0),
        "beam_dirs": plant(jax.random.randint(key_of[3], (B,), 0, DIRS), jax.random.fold_in(key_of[3], 1), 0, DIRS - 1).astype(jnp.int32),
        "chan_table": jax.random.permutation(key_of[4], C).astype(jnp.int32),
    }


loading_level = 0.1
full_turn = 2.0 * math.pi

def dft_tables(chan_table):
    frame_width = 2 * C
    phase_index = jnp.remainder(chan_table[:, None] * jnp.arange(frame_width, dtype=jnp.int32)[None, :], frame_width)
    angles = phase_index.astype(jnp.float32) * (full_turn / frame_width)
    return jnp.stack([jnp.cos(angles), -jnp.sin(angles)], axis=1)

def filter_block(station_block, filter_taps):
    snap_count = station_block.shape[2] - (TAPS - 1)
    widened = station_block.astype(jnp.float32)
    summed = jnp.zeros((station_block.shape[0], station_block.shape[1], snap_count), jnp.float32)
    for tap_index in range(TAPS):
        offset = TAPS - 1 - tap_index
        summed = summed + filter_taps[tap_index][None, :, None] * widened[:, :, offset:offset + snap_count]
    return summed

def channelize(filtered, dft_table):
    return jnp.einsum('jap,spt->jast', dft_table, filtered, precision=lax.Precision.HIGHEST).astype(jnp.bfloat16)

def halves(gram_full):
    half_size = gram_full.shape[-1] // 2
    sym_part = gram_full[..., :half_size, :half_size] + gram_full[..., half_size:, half_size:]
    skew_part = gram_full[..., half_size:, :half_size] - gram_full[..., :half_size, half_size:]
    return (sym_part, skew_part)

def assemble(sym_part, skew_part):
    upper_rows = jnp.concatenate([sym_part, -skew_part], axis=-1)
    bottom = jnp.concatenate([skew_part, sym_part], axis=-1)
    return jnp.concatenate([upper_rows, bottom], axis=-2)

def steering(positions, beam_dirs, channel):
    bearing = beam_dirs.astype(jnp.float32) * (full_turn / DIRS)
    frequency = 1.0 + channel.astype(jnp.float32) / C
    path_delay = positions[0][:, None] * jnp.cos(bearing)[None, :] + positions[1][:, None] * jnp.sin(bearing)[None, :]
    phases = full_turn * frequency * path_delay
    return jnp.concatenate([jnp.cos(phases), jnp.sin(phases)], axis=0)

def solve_weights(factor, steer):
    whitened = jax.scipy.linalg.solve_triangular(factor, steer, lower=True)
    column_power = lax.optimization_barrier(jnp.sum(whitened * whitened, axis=0))
    solved = jax.scipy.linalg.solve_triangular(factor, whitened, lower=True, trans=1)
    return (solved / jnp.sqrt(column_power)[None, :]).astype(jnp.bfloat16)

def mixing(weights):
    half_size = weights.shape[0] // 2
    swapped = jnp.concatenate([-weights[half_size:], weights[:half_size]], axis=0)
    return jnp.concatenate([weights.T, swapped.T], axis=0)

def reference(voltages, filter_taps, positions, beam_dirs, chan_table):
    dft_table = dft_tables(chan_table)
    padded = jnp.pad(voltages, ((0, 0), (0, 0), (TAPS - 1, 0)))
    station_blocks = padded.reshape(N_STN, S // N_STN, 2 * C, SNAPS + TAPS - 1)
    spectra = lax.map(lambda station_block: channelize(filter_block(station_block, filter_taps), dft_table), station_blocks)
    spectra = jnp.transpose(spectra, (1, 2, 0, 3, 4)).reshape(C, 2 * S, SNAPS)
    identity = jnp.eye(2 * S, dtype=jnp.float32)

    def one_channel(channel_item):
        stacked, channel = channel_item
        gram_full = jnp.dot(stacked.astype(jnp.float32), stacked.T.astype(jnp.float32), preferred_element_type=jnp.float32)
        sym_part, skew_part = halves(gram_full)
        covariance = assemble(sym_part, skew_part) / SNAPS + loading_level * identity
        factor = jnp.linalg.cholesky(covariance)
        weights = solve_weights(factor, steering(positions, beam_dirs, channel))
        mix_matrix = mixing(weights)
        beam_out = jnp.dot(mix_matrix.astype(jnp.float32), stacked.astype(jnp.float32), preferred_element_type=jnp.float32)
        return beam_out.astype(jnp.bfloat16).reshape(2, B, SNAPS)
    return lax.map(one_channel, (spectra, chan_table))
```

```python
import functools
import math

import jax
import jax.numpy as jnp
import numpy as np
from jax import lax
from jax.experimental import pallas as pl
from jax.experimental.pallas import tpu as pltpu
from jax.sharding import PartitionSpec as P

DIRS = 360
LANES = 128
GROUP = 8
PIVOTS = 16

loading_level = 0.1
full_turn = 2.0 * math.pi
NT = (((1,), (1,)), ((), ()))
TN = (((0,), (0,)), ((), ()))
f32, bf16 = jnp.float32, jnp.bfloat16


def split_in_two(value):
    high = value.astype(bf16)
    return high, (value - high.astype(f32)).astype(bf16)


def block_tables(channels):
    width = 2 * channels
    phase = (np.arange(channels)[:, None] * np.arange(width)[None, :]) % width
    angles = phase * (full_turn / width)
    parts = np.stack([np.cos(angles), -np.sin(angles)], axis=1).astype(np.float32)
    blocks = np.einsum("kap,st->kastp", parts, np.eye(GROUP, dtype=np.float32))
    blocks = blocks.reshape(channels, 2 * GROUP, GROUP * width)
    high = blocks.astype(bf16)
    return high, (blocks - high.astype(np.float32)).astype(bf16)


def merged_rows(pieces):
    if all(piece.shape[0] % 16 == 0 for piece in pieces):
        return jnp.concatenate(pieces, axis=0)
    return jnp.concatenate([piece.astype(f32) for piece in pieces], axis=0).astype(bf16)


def channelize_kernel(slot, slots, owners, chans, volts, halo, taps, table_high, table_low, *refs):
    outs, (dft, before, high, low) = refs[:owners], refs[owners:]
    stations, width, chunk = volts.shape
    rows = 2 * GROUP

    @pl.when(pl.program_id(0) == 0)
    def _():
        before[...] = halo[...]
        for index in range(owners):
            channel = chans[index, slot]
            dft[pl.ds(index * rows, rows), :] = table_high[channel]
            dft[pl.ds((owners + index) * rows, rows), :] = table_low[channel]

    tap = [jnp.broadcast_to(taps[:, m : m + 1], (width, LANES)) for m in range(8)]
    tap = [jnp.concatenate([one] * (chunk // LANES + 1), axis=1) for one in tap]
    groups = []
    for group in range(stations // GROUP):
        for member in range(GROUP):
            station = group * GROUP + member
            now = jnp.concatenate([before[station], volts[station]], axis=1).astype(f32)
            shifted = [now] + [pltpu.roll(now, m, axis=1) for m in (1, 2, 3)]
            near = sum(tap[m] * shifted[m] for m in range(4))
            far = sum(tap[4 + m] * shifted[m] for m in range(4))
            filtered = (near + pltpu.roll(far, 4, axis=1))[:, LANES:]
            top, rest = split_in_two(filtered)
            high[pl.ds(member * width, width), :] = top
            low[pl.ds(member * width, width), :] = rest
            before[station] = volts[station, :, chunk - LANES :]
        both = jnp.dot(dft[...], high[...], preferred_element_type=f32)
        cross = jnp.dot(dft[: owners * rows], low[...], preferred_element_type=f32)
        groups.append(both[: owners * rows] + (both[owners * rows :] + cross))
    for index in range(owners):
        for part in range(2):
            first = index * rows + part * GROUP
            piece = [one[first : first + GROUP] for one in groups]
            outs[index][part] = jnp.concatenate(piece, axis=0).astype(bf16)


def channelize(slot, slots, chans, volts, halo, taps, tables):
    stations, width, snaps = volts.shape
    owners = chans.shape[0]
    chunk = min(snaps, 512)
    kernel = functools.partial(channelize_kernel, slot, slots, owners)
    whole = lambda shape: pl.BlockSpec(shape, lambda t, c: (0,) * len(shape))
    out = jax.ShapeDtypeStruct((2, stations, snaps), bf16)
    return pl.pallas_call(
        kernel,
        grid_spec=pltpu.PrefetchScalarGridSpec(
            num_scalar_prefetch=1,
            grid=(snaps // chunk,),
            in_specs=[
                pl.BlockSpec((stations, width, chunk), lambda t, c: (0, 0, t)),
                whole(halo.shape),
                whole(taps.shape),
                whole(tables[0].shape),
                whole(tables[1].shape),
            ],
            out_specs=[pl.BlockSpec((2, stations, chunk), lambda t, c: (0, 0, t))] * owners,
            scratch_shapes=[
                pltpu.VMEM((2 * owners * 2 * GROUP, GROUP * width), bf16),
                pltpu.VMEM((stations, width, LANES), bf16),
                pltpu.VMEM((GROUP * width, chunk), bf16),
                pltpu.VMEM((GROUP * width, chunk), bf16),
            ],
        ),
        out_shape=[out] * owners,
        compiler_params=pltpu.CompilerParams(vmem_limit_bytes=32 << 20),
        cost_estimate=pl.CostEstimate(flops=2 * 10**9, bytes_accessed=4 << 20, transcendentals=0),
        name="channelize",
    )(chans, volts, halo, taps, *tables)


def gram_kernel(owners, *refs):
    blocks, out, total = refs[:owners], refs[owners], refs[owners + 1]
    half = owners * blocks[0].shape[1]
    stacked = merged_rows([one[part] for part in range(2) for one in blocks])
    gram = lax.dot_general(stacked, stacked, NT, preferred_element_type=f32)

    @pl.when(pl.program_id(0) == 0)
    def _():
        total[...] = gram

    @pl.when(pl.program_id(0) > 0)
    def _():
        total[...] += gram

    @pl.when(pl.program_id(0) == pl.num_programs(0) - 1)
    def _():
        sym_part = total[:half, :half] + total[half:, half:]
        skew_part = total[half:, :half] - total[:half, half:]
        row = lax.broadcasted_iota(jnp.int32, (half, half), 0)
        column = lax.broadcasted_iota(jnp.int32, (half, half), 1)
        out[...] = jnp.where(row >= column, sym_part, skew_part)


def packed_gram(blocks):
    _, stations, snaps = blocks[0].shape
    half = len(blocks) * stations
    chunk = min(snaps, 1024)
    return pl.pallas_call(
        functools.partial(gram_kernel, len(blocks)),
        grid=(snaps // chunk,),
        in_specs=[pl.BlockSpec((2, stations, chunk), lambda t: (0, 0, t))] * len(blocks),
        out_specs=pl.BlockSpec((half, half), lambda t: (0, 0)),
        out_shape=jax.ShapeDtypeStruct((half, half), f32),
        scratch_shapes=[pltpu.VMEM((2 * half, 2 * half), f32)],
        compiler_params=pltpu.CompilerParams(vmem_limit_bytes=32 << 20),
        cost_estimate=pl.CostEstimate(flops=3 * 10**8, bytes_accessed=1 << 20, transcendentals=0),
        name="gram",
    )(*blocks)


def dot(a, b, dims=(((1,), (0,)), ((), ()))):
    return lax.dot_general(a, b, dims, precision=lax.Precision.HIGHEST, preferred_element_type=f32)


def eliminate(real, imag, pivots):
    half = real.shape[0]
    for first in range(0, half, pivots):
        row_r, row_i = real[first : first + pivots], imag[first : first + pivots]
        side = jnp.concatenate(
            [
                jnp.concatenate([row_r[:, :half], -row_i[:, :half]], axis=1),
                jnp.concatenate([row_i[:, :half], row_r[:, :half]], axis=1),
            ],
            axis=0,
        )
        tile = first // LANES * LANES
        index = lax.broadcasted_iota(jnp.int32, row_r.shape, 0)
        lane = lax.broadcasted_iota(jnp.int32, row_r.shape, 1) - first
        inside = (lane >= 0) & (lane < pivots)
        row_r = jnp.concatenate([row_r[:, tile : tile + LANES], jnp.where(inside, jnp.where(lane == index, -1.0, 0.0), row_r)], axis=1)
        row_i = jnp.concatenate([row_i[:, tile : tile + LANES], jnp.where(inside, 0.0, row_i)], axis=1)
        index = lax.broadcasted_iota(jnp.int32, row_r.shape, 0)
        for step in range(pivots):
            lane = first - tile + step
            col_r = jnp.broadcast_to(row_r[:, lane : lane + 1], row_r.shape)
            col_i = jnp.broadcast_to(row_i[:, lane : lane + 1], row_i.shape)
            scale = 1.0 / jnp.broadcast_to(col_r[step : step + 1], row_r.shape)
            pick_r = jnp.broadcast_to(row_r[step : step + 1], row_r.shape) * scale
            pick_i = jnp.broadcast_to(row_i[step : step + 1], row_i.shape) * scale
            here = index == step
            row_r, row_i = (
                jnp.where(here, pick_r, row_r - (col_r * pick_r - col_i * pick_i)),
                jnp.where(here, pick_i, row_i - (col_r * pick_i + col_i * pick_r)),
            )
        row_r, row_i = row_r[:, LANES:], row_i[:, LANES:]
        update = dot(side, jnp.concatenate([row_r, row_i], axis=0), TN)
        rank = lax.broadcasted_iota(jnp.int32, real.shape, 0) - first
        own = (rank >= 0) & (rank < pivots)
        lane = lax.broadcasted_iota(jnp.int32, real.shape, 1) - first
        gone = (lane >= 0) & (lane < pivots)
        spread = lambda piece: jnp.concatenate([piece] * (half // pivots), axis=0)
        real = jnp.where(own, spread(row_r), jnp.where(gone, 0.0, real) - update[:half])
        imag = jnp.where(own, spread(row_i), jnp.where(gone, 0.0, imag) - update[half:])
    return real, imag


def beams_kernel(owners, segments, snap_total, has_earlier, *refs):
    grams, steer, blocks = refs[:segments], refs[segments], refs[segments + 1 : segments + 1 + owners]
    out, mix = refs[-2], refs[-1]
    half = grams[0].shape[0]

    @pl.when(pl.program_id(0) == 0)
    def _():
        packed = sum(one[...] for one in grams) * (1.0 / snap_total)
        row = lax.broadcasted_iota(jnp.int32, (half, half), 0)
        column = lax.broadcasted_iota(jnp.int32, (half, half), 1)
        turned = packed.T
        real = jnp.where(row >= column, packed, turned)
        real = jnp.where(row == column, real + loading_level, real)
        imag = jnp.where(row < column, packed, jnp.where(row > column, -turned, 0.0))
        steer_r, steer_i = steer[:half], steer[half:]
        real, imag = eliminate(
            jnp.concatenate([real, steer_r], axis=1),
            jnp.concatenate([imag, steer_i], axis=1),
            PIVOTS,
        )
        solved_r, solved_i = real[:, half:], imag[:, half:]
        power = jnp.sum(steer_r * solved_r + steer_i * solved_i, axis=0, keepdims=True)
        scale = 1.0 / jnp.sqrt(power)
        weight_r, weight_i = solved_r * scale, solved_i * scale
        upper = jnp.concatenate([weight_r.T, weight_i.T], axis=1)
        lower = jnp.concatenate([-weight_i.T, weight_r.T], axis=1)
        mix[...] = jnp.concatenate([upper, lower], axis=0).astype(bf16)

    stacked = merged_rows([one[part] for part in range(2) for one in blocks])
    beams = jnp.dot(mix[...], stacked, preferred_element_type=f32).astype(bf16)
    count = mix.shape[0] // 2
    out[0, 0] = beams[:count]
    out[0, 1] = beams[count:]


def beams(slot, slots, snap_total, grams, steer, blocks, earlier):
    _, stations, snaps = blocks[0].shape
    half = len(blocks) * stations
    count = steer.shape[1]
    chunk = min(snaps, 1024)
    whole = lambda shape: pl.BlockSpec(shape, lambda t: (0,) * len(shape))
    kernel = functools.partial(beams_kernel, len(blocks), len(grams), snap_total, earlier is not None)
    operands = [*grams, steer, *blocks]
    specs = [whole((half, half))] * len(grams) + [whole(steer.shape)]
    specs += [pl.BlockSpec((2, stations, chunk), lambda t: (0, 0, t))] * len(blocks)
    aliases = {}
    if earlier is not None:
        aliases = {len(operands): 0}
        operands.append(earlier)
        specs.append(pl.BlockSpec(memory_space=pl.ANY))
    return pl.pallas_call(
        kernel,
        grid=(snaps // chunk,),
        in_specs=specs,
        out_specs=pl.BlockSpec((1, 2, count, chunk), lambda t: (slot, 0, 0, t)),
        out_shape=jax.ShapeDtypeStruct((slots, 2, count, snaps), bf16),
        scratch_shapes=[pltpu.VMEM((2 * count, 2 * half), bf16)],
        input_output_aliases=aliases,
        compiler_params=pltpu.CompilerParams(vmem_limit_bytes=48 << 20),
        cost_estimate=pl.CostEstimate(flops=10**10, bytes_accessed=3 << 20, transcendentals=0),
        name="beams",
    )(*operands)


def partners(value, axis, distance):
    length = lax.axis_size(axis)
    return lax.ppermute(value, axis, [(i, i ^ distance) for i in range(length)])


def segment_sums(packed):
    length = lax.axis_size("seg")
    if length <= 4:
        return [packed] + [partners(packed, "seg", d) for d in range(1, length)]
    distance = 1
    while distance < length:
        packed = packed + partners(packed, "seg", distance)
        distance *= 2
    return [packed]


def steering(positions, beam_dirs, channel, channels):
    bearing = beam_dirs.astype(f32) * (full_turn / DIRS)
    frequency = 1.0 + channel.astype(f32) / channels
    path_delay = (
        positions[0][:, None] * jnp.cos(bearing)[None, :]
        + positions[1][:, None] * jnp.sin(bearing)[None, :]
    )
    phases = full_turn * frequency * path_delay
    return jnp.concatenate([jnp.cos(phases), jnp.sin(phases)], axis=0)


def on_device(voltages, filter_taps, positions, beam_dirs, chan_table):
    stations, width, snaps = voltages.shape
    channels = chan_table.shape[0]
    owners = lax.axis_size("stn")
    segments = lax.axis_size("seg")
    slots = channels // owners
    snap_total = snaps * segments
    halo = lax.ppermute(
        voltages[:, :, snaps - LANES :], "seg", [(i, i + 1) for i in range(segments - 1)]
    )
    order = lax.axis_index("stn") ^ jnp.arange(owners, dtype=jnp.int32)
    chans = chan_table.reshape(owners, slots)[order]
    places = positions.reshape(2, owners, stations)[:, order].reshape(2, owners * stations)
    steer = [steering(places, beam_dirs, chans[0, slot], channels) for slot in range(slots)]
    tables = block_tables(channels)
    taps = filter_taps.T
    result = None
    distances = sorted(range(1, owners), key=lambda d: (d < owners // 2, d))
    spectra = [channelize(s, slots, chans, voltages, halo, taps, tables) for s in range(slots)]
    for slot in range(slots):
        mine = spectra[slot]
        arrived = {d: partners(mine[d], "stn", d) for d in distances}
        blocks = [mine[0]] + [arrived[d] for d in range(1, owners)]
        grams = segment_sums(packed_gram(blocks))
        result = beams(slot, slots, snap_total, grams, steer[slot], blocks, result)
    return result


def solution(mesh):
    return jax.shard_map(
        on_device,
        mesh=mesh,
        in_specs=(P("stn", None, "seg"), P(), P(), P(), P()),
        out_specs=P("stn", None, None, "seg"),
        check_vma=False,
    )
```

```python
import functools
import math

import jax
import jax.numpy as jnp
from jax import lax
from jax.experimental import pallas as pl
from jax.experimental.pallas import tpu as pltpu
from jax.sharding import PartitionSpec as P

DIRS = 360
LANES = 128
GROUP = 8
PIVOTS = 16
AT_ONCE = 8
VMEM_BYTES = 16 << 20
GRAM_VMEM = 8 << 20
BEAMS_VMEM = 12 << 20

loading_level = 0.1
full_turn = 2.0 * math.pi
NT = (((1,), (1,)), ((), ()))
TN = (((0,), (0,)), ((), ()))
f32, bf16 = jnp.float32, jnp.bfloat16


def split_in_two(value):
    high = value.astype(bf16)
    return high, (value - high.astype(f32)).astype(bf16)


def merged_rows(pieces):
    if all(piece.shape[0] % 16 == 0 for piece in pieces):
        return jnp.concatenate(pieces, axis=0)
    return jnp.concatenate([piece.astype(f32) for piece in pieces], axis=0).astype(bf16)


def dft_rows(channels, width):
    shape = (2 * len(channels), GROUP * width)
    row = lax.broadcasted_iota(jnp.int32, shape, 0)
    lane = lax.broadcasted_iota(jnp.int32, shape, 1)
    channel = jnp.zeros(shape, jnp.int32)
    for index, one in enumerate(channels):
        channel = jnp.where(row // 2 == index, one, channel)
    angle = lax.rem(channel * lax.rem(lane, width), width).astype(f32) * (full_turn / width)
    values = jnp.where(row % 2 == 0, jnp.cos(angle), -jnp.sin(angle))
    shape = (GROUP, GROUP * width)
    own = lax.broadcasted_iota(jnp.int32, shape, 1) // width == lax.broadcasted_iota(jnp.int32, shape, 0)
    spread = [jnp.where(own, jnp.broadcast_to(values[i : i + 1], shape), 0.0) for i in range(2 * len(channels))]
    return jnp.concatenate(spread, axis=0)


def channelize_kernel(owners, first_slot, slots, part, joined, *refs):
    count = owners * slots
    has_halo = part != "second"
    chans_in, volts, taps_in = refs[:3]
    others = refs[3 + has_halo : 3 + has_halo + joined]
    outs = refs[3 + has_halo + joined : len(refs) - 10]
    dft, held, high, low, chans, taps, sems, chans_sem, taps_sem, halo_sem = refs[-10:]
    stations, width, snaps = volts.shape
    chunk = held.shape[2] - LANES
    tap_count = taps.shape[0]
    step = tap_count // 2
    rows = 2 * GROUP
    half = count * rows
    pieces = sems.shape[0]
    piece = stations // pieces
    small = [pltpu.make_async_copy(chans_in, chans, chans_sem), pltpu.make_async_copy(taps_in, taps, taps_sem)]
    if has_halo:
        small.append(pltpu.make_async_copy(refs[3], held.at[:, :, :LANES], halo_sem))
    copies = []
    for index in range(pieces):
        members = pl.ds(index * piece, piece)
        if has_halo:
            source, target = volts.at[members, :, :chunk], held.at[members, :, LANES:]
        else:
            source, target = volts.at[members, :, snaps - chunk - LANES :], held.at[members]
        copies.append(pltpu.make_async_copy(source, target, sems.at[index]))
    for copy in small + copies:
        copy.start()
    for copy in small:
        copy.wait()

    me = lax.axis_index("stn")
    every = chans.shape[0] // owners
    table = dft_rows([chans[(me ^ d) * every + first_slot + slot] for slot in range(slots) for d in range(owners)], width)
    dft[:half], dft[half:] = split_in_two(table)
    columns = taps[...].T
    tap = [jnp.broadcast_to(columns[:, m : m + 1], (width, chunk + LANES)) for m in range(tap_count)]
    results = []
    for station in range(stations):
        if station % piece == 0:
            copies[station // piece].wait()
        now = held[station]
        shifted = [(pltpu.roll(now, m, axis=1) if m else now).astype(f32) for m in range(step)]
        near = sum(tap[m] * shifted[m] for m in range(step))
        far = sum(tap[step + m] * shifted[m] for m in range(step))
        filtered = (near + pltpu.roll(far, step, axis=1))[:, LANES:]
        member = station % GROUP
        high[pl.ds(member * width, width), :], low[pl.ds(member * width, width), :] = split_in_two(filtered)
        if member == GROUP - 1:
            both = jnp.dot(dft[...], high[...], preferred_element_type=f32)
            cross = jnp.dot(dft[:half], low[...], preferred_element_type=f32)
            results.append(both[:half] + (both[half:] + cross))
    for index in range(count):
        for real in range(2):
            first = index * rows + real * GROUP
            outs[index][real, :, :chunk] = jnp.concatenate([one[first : first + GROUP] for one in results], axis=0).astype(bf16)
        if index < joined:
            outs[index][:, :, chunk:] = others[index][...]


def channelize(owners, first_slot, slots, part, chans, volts, taps, halo=None, joined=()):
    stations, width, snaps = volts.shape
    count = owners * slots
    chunk = snaps if part == "whole" else snaps // 2
    pieces = max(stations // 4, 1)
    out_shape = [jax.ShapeDtypeStruct((2, stations, snaps if i < len(joined) else chunk), bf16) for i in range(count)]
    operands = [pltpu.with_memory_space_constraint(one, pltpu.HBM) for one in (chans, volts, taps)]
    operands += ([] if halo is None else [halo]) + list(joined)
    return pl.pallas_call(
        functools.partial(channelize_kernel, owners, first_slot, slots, part, len(joined)),
        in_specs=[pl.BlockSpec(memory_space=pltpu.HBM)] * 3
        + [pl.BlockSpec(memory_space=pl.ANY)] * (halo is not None)
        + [pl.BlockSpec(memory_space=pltpu.VMEM)] * len(joined),
        out_specs=[pl.BlockSpec(memory_space=pltpu.VMEM)] * len(out_shape),
        out_shape=out_shape,
        scratch_shapes=[
            pltpu.VMEM((4 * count * GROUP, GROUP * width), bf16),
            pltpu.VMEM((stations, width, chunk + LANES), bf16),
            pltpu.VMEM((GROUP * width, chunk), bf16),
            pltpu.VMEM((GROUP * width, chunk), bf16),
            pltpu.SMEM(chans.shape, jnp.int32),
            pltpu.VMEM(taps.shape, f32),
            pltpu.SemaphoreType.DMA((pieces,)),
            pltpu.SemaphoreType.DMA(()),
            pltpu.SemaphoreType.DMA(()),
            pltpu.SemaphoreType.DMA(()),
        ],
        compiler_params=pltpu.CompilerParams(vmem_limit_bytes=VMEM_BYTES),
        cost_estimate=pl.CostEstimate(flops=4 * 10**9, bytes_accessed=3 << 20, transcendentals=0),
        name="channelize_" + part,
    )(*operands)


def stacked_rows(counts, refs):
    rows = []
    for part in range(2):
        at = 0
        for count in counts:
            rows.append(jnp.concatenate([one[part] for one in refs[at : at + count]], axis=1))
            at += count
    return merged_rows(rows)


def gram_kernel(counts, *refs):
    out = refs[-1]
    half = out.shape[0]
    stacked = stacked_rows(counts, refs[:-1])
    gram = lax.dot_general(stacked, stacked, NT, preferred_element_type=f32)
    sym_part = gram[:half, :half] + gram[half:, half:]
    skew_part = gram[half:, :half] - gram[:half, half:]
    row = lax.broadcasted_iota(jnp.int32, (half, half), 0)
    column = lax.broadcasted_iota(jnp.int32, (half, half), 1)
    out[...] = jnp.where(row >= column, sym_part, skew_part)


def packed_gram(blocks):
    half = len(blocks) * blocks[0][0].shape[1]
    operands = [one for block in blocks for one in block]
    return pl.pallas_call(
        functools.partial(gram_kernel, [len(block) for block in blocks]),
        in_specs=[pl.BlockSpec(memory_space=pltpu.VMEM)] * len(operands),
        out_specs=pl.BlockSpec(memory_space=pltpu.VMEM),
        out_shape=jax.ShapeDtypeStruct((half, half), f32),
        compiler_params=pltpu.CompilerParams(vmem_limit_bytes=GRAM_VMEM),
        cost_estimate=pl.CostEstimate(flops=3 * 10**8, bytes_accessed=1 << 20, transcendentals=0),
        name="gram",
    )(*operands)


def split_in_three(value):
    high, rest = value.astype(bf16), value
    rest = rest - high.astype(f32)
    middle = rest.astype(bf16)
    return high, middle, (rest - middle.astype(f32)).astype(bf16)


def deep_dot(left, right):
    a, b = split_in_three(left), split_in_three(right)
    left = jnp.concatenate([a[0], a[0], a[1], a[1], a[0], a[2]], axis=0)
    right = jnp.concatenate([b[0], b[1], b[0], b[1], b[2], b[0]], axis=0)
    return lax.dot_general(left, right, TN, preferred_element_type=f32)


def sweep_rows(row_r, row_i, lanes, at_once):
    count, width = row_r.shape
    narrow = (count, LANES)
    tiles = width // LANES
    index, index_wide = (lax.broadcasted_iota(jnp.int32, shape, 0) for shape in (narrow, (count, width)))
    repeated = lambda value: jnp.concatenate([value] * tiles, axis=1)
    for start in range(0, count, at_once):
        fetched = lanes[start : start + at_once]
        col_r = [jnp.broadcast_to(row_r[:, lane : lane + 1], narrow) for lane in fetched]
        col_i = [jnp.broadcast_to(row_i[:, lane : lane + 1], narrow) for lane in fetched]
        for j in range(len(fetched)):
            step = start + j
            spread = lambda value: jnp.broadcast_to(value[step : step + 1], value.shape)
            a, b = col_r[j], col_i[j]
            scale = 1.0 / spread(a)

            def swept(real, imag, here, a, b, scale):
                pick_r, pick_i = spread(real) * scale, spread(imag) * scale
                return (
                    jnp.where(here, pick_r, real - (a * pick_r - b * pick_i)),
                    jnp.where(here, pick_i, imag - (a * pick_i + b * pick_r)),
                )

            for later in range(j + 1, len(fetched)):
                col_r[later], col_i[later] = swept(col_r[later], col_i[later], index == step, a, b, scale)
            row_r, row_i = swept(row_r, row_i, index_wide == step, repeated(a), repeated(b), repeated(scale))
    return row_r, row_i


def eliminate(real, imag, pivots, at_once):
    half = real.shape[0]
    rank = lax.broadcasted_iota(jnp.int32, real.shape, 0)
    lane = lax.broadcasted_iota(jnp.int32, real.shape, 1)
    for first in range(0, half, pivots):
        last = first + pivots
        row_r, row_i = real[first:last], imag[first:last]
        side = jnp.concatenate(
            [
                jnp.concatenate([row_r[:, :half], -row_i[:, :half]], axis=1),
                jnp.concatenate([row_i[:, :half], row_r[:, :half]], axis=1),
            ],
            axis=0,
        )
        tile = first // LANES * LANES
        inside = (lane[first:last] >= first) & (lane[first:last] < last)
        minus_one = jnp.where(rank[first:last] == lane[first:last], -1.0, 0.0)
        row_r, row_i = sweep_rows(
            jnp.concatenate([row_r[:, tile : tile + LANES], jnp.where(inside, minus_one, row_r)], axis=1),
            jnp.concatenate([row_i[:, tile : tile + LANES], jnp.where(inside, 0.0, row_i)], axis=1),
            range(first - tile, last - tile),
            at_once,
        )
        row_r, row_i = row_r[:, LANES:], row_i[:, LANES:]
        update = deep_dot(side, jnp.concatenate([row_r, row_i], axis=0))
        own = (rank >= first) & (rank < last)
        gone = (lane >= first) & (lane < last)
        spread = lambda piece: jnp.concatenate([piece] * (half // pivots), axis=0)
        real = jnp.where(own, spread(row_r), jnp.where(gone, 0.0, real) - update[:half])
        imag = jnp.where(own, spread(row_i), jnp.where(gone, 0.0, imag) - update[half:])
    return real, imag


def beams_kernel(segments, snap_total, counts, *refs):
    grams, steer, blocks = refs[:segments], refs[segments], refs[segments + 1 : segments + 1 + sum(counts)]
    out = refs[-1]
    half = grams[0].shape[0]
    packed = sum(one[...] for one in grams) * (1.0 / snap_total)
    row = lax.broadcasted_iota(jnp.int32, (half, half), 0)
    column = lax.broadcasted_iota(jnp.int32, (half, half), 1)
    turned = packed.T
    real = jnp.where(row >= column, packed, turned)
    real = jnp.where(row == column, real + loading_level, real)
    imag = jnp.where(row < column, packed, jnp.where(row > column, -turned, 0.0))
    steer_r, steer_i = steer[:half], steer[half:]
    real, imag = eliminate(
        jnp.concatenate([real, steer_r], axis=1),
        jnp.concatenate([imag, steer_i], axis=1),
        PIVOTS,
        AT_ONCE,
    )
    solved_r, solved_i = real[:, half:], imag[:, half:]
    power = jnp.sum(steer_r * solved_r + steer_i * solved_i, axis=0, keepdims=True)
    scale = 1.0 / jnp.sqrt(power)
    weight_r, weight_i = (solved_r * scale).T, (solved_i * scale).T
    upper = jnp.concatenate([weight_r, weight_i], axis=1)
    lower = jnp.concatenate([-weight_i, weight_r], axis=1)
    mix = jnp.concatenate([upper, lower], axis=0).astype(bf16)
    count = steer.shape[1]
    mixed = jnp.dot(mix, stacked_rows(counts, blocks), preferred_element_type=f32).astype(bf16)
    out[0, 0] = mixed[:count]
    out[0, 1] = mixed[count:]


def beams(slot, slots, snap_total, grams, steer, blocks, earlier):
    snaps = sum(one.shape[2] for one in blocks[0])
    count = steer.shape[1]
    operands = [*grams, steer] + [one for block in blocks for one in block]
    specs = [pl.BlockSpec(memory_space=pltpu.VMEM)] * len(operands)
    aliases = {}
    if earlier is not None:
        aliases = {len(operands): 0}
        operands.append(earlier)
        specs.append(pl.BlockSpec(memory_space=pl.ANY))
    return pl.pallas_call(
        functools.partial(beams_kernel, len(grams), snap_total, [len(block) for block in blocks]),
        grid=(1,),
        in_specs=specs,
        out_specs=pl.BlockSpec((1, 2, count, snaps), lambda i: (slot, 0, 0, 0)),
        out_shape=jax.ShapeDtypeStruct((slots, 2, count, snaps), bf16),
        input_output_aliases=aliases,
        compiler_params=pltpu.CompilerParams(vmem_limit_bytes=BEAMS_VMEM),
        cost_estimate=pl.CostEstimate(flops=10**10, bytes_accessed=3 << 20, transcendentals=0),
        name="beams",
    )(*operands)


def partners(value, axis, distance):
    length = lax.axis_size(axis)
    return lax.ppermute(value, axis, [(i, i ^ distance) for i in range(length)])


def segment_sums(packed, hurried):
    length = lax.axis_size("seg")
    if hurried and length <= 4:
        return [packed] + [partners(packed, "seg", d) for d in range(1, length)]
    distance = 1
    while distance < length:
        packed = packed + partners(packed, "seg", distance)
        distance *= 2
    return [packed]


def steering(positions, beam_dirs, channel, channels):
    bearing = beam_dirs.astype(f32) * (full_turn / DIRS)
    frequency = 1.0 + channel.astype(f32) / channels
    path_delay = (
        positions[0][:, None] * jnp.cos(bearing)[None, :]
        + positions[1][:, None] * jnp.sin(bearing)[None, :]
    )
    phases = full_turn * frequency * path_delay
    return jnp.concatenate([jnp.cos(phases), jnp.sin(phases)], axis=0)


def after(value, earlier):
    return lax.optimization_barrier((value, earlier))


def on_device(voltages, filter_taps, positions, beam_dirs, chan_table):
    stations, width, snaps = voltages.shape
    channels = chan_table.shape[0]
    owners = lax.axis_size("stn")
    segments = lax.axis_size("seg")
    slots = channels // owners
    snap_total = snaps * segments
    near, far = list(range(1, owners // 2)), list(range(owners // 2, owners))
    halo = lax.ppermute(voltages[:, :, snaps - LANES :], "seg", [(i, i + 1) for i in range(segments - 1)])
    second = channelize(owners, 0, 1, "second", chan_table, voltages, filter_taps)
    late = {d: partners(second[d], "stn", d) for d in far}
    first = channelize(owners, 0, 1, "first", chan_table, voltages, filter_taps, halo, second[: owners // 2])
    early = {d: partners(first[d], "stn", d) for d in far}
    own, whole = first[0], {}
    for index, d in enumerate(near):
        value, late[far[index]] = after(first[d], late[far[index]])
        whole[d] = partners(value, "stn", d)
    blocks = [[own]] + [[whole[d]] for d in near] + [[early[d], late[d]] for d in far]
    result = None
    if slots > 1:
        halo, blocks[0][0] = after(halo, blocks[0][0])
        rest = channelize(owners, 1, slots - 1, "whole", chan_table, voltages, filter_taps, halo)
    if near:
        (positions, beam_dirs, chan_table), blocks[near[-1]][0] = after(
            (positions, beam_dirs, chan_table), blocks[near[-1]][0]
        )
    order = lax.axis_index("stn") ^ jnp.arange(owners, dtype=jnp.int32)
    places = positions.reshape(2, owners, stations)[:, order].reshape(2, owners * stations)
    chans = lax.dynamic_slice_in_dim(chan_table, lax.axis_index("stn") * slots, slots)
    for slot in range(slots):
        steer = steering(places, beam_dirs, chans[slot], channels)
        following = [None] * owners
        if slot + 1 < slots:
            sent = rest[slot * owners : (slot + 1) * owners]
            following[0] = [sent[0]]
            gates = [near[-1]] + far if near else far
            for index, d in enumerate(far):
                gate = blocks[gates[index]]
                value, gate[0] = after(sent[d], gate[0])
                following[d] = [partners(value, "stn", d)]
        grams = segment_sums(packed_gram(blocks), slot + 1 == slots)
        if slot + 1 < slots:
            for d in near:
                value, grams[0] = after(sent[d], grams[0])
                following[d] = [partners(value, "stn", d)]
        result = beams(slot, slots, snap_total, grams, steer, blocks, result)
        if slot + 1 < slots:
            blocks, result = after(following, result)
    return result


def solution(mesh):
    return jax.shard_map(
        on_device,
        mesh=mesh,
        in_specs=(P("stn", None, "seg"), P(), P(), P(), P()),
        out_specs=P("stn", None, None, "seg"),
        check_vma=False,
    )
```

```python
import functools
import math

import jax
import jax.numpy as jnp
from jax import lax
from jax.experimental import pallas as pl
from jax.experimental.pallas import tpu as pltpu
from jax.sharding import PartitionSpec as P

DIRS = 360
LANES = 128
GROUP = 8
PIVOTS = 16
QUICK = pl.CostEstimate(flops=1000, bytes_accessed=1000, transcendentals=0)
AT_ONCE = 4
VMEM_BYTES = 16 << 20
GRAM_VMEM = 8 << 20
BEAMS_VMEM = 12 << 20

loading_level = 0.1
full_turn = 2.0 * math.pi
NN = (((1,), (0,)), ((), ()))
NT = (((1,), (1,)), ((), ()))
TN = (((0,), (0,)), ((), ()))
f32, bf16 = jnp.float32, jnp.bfloat16


def split_in_two(value):
    high = value.astype(bf16)
    return high, (value - high.astype(f32)).astype(bf16)


def merged_rows(pieces):
    if all(piece.shape[0] % 16 == 0 for piece in pieces):
        return jnp.concatenate(pieces, axis=0)
    return jnp.concatenate([piece.astype(f32) for piece in pieces], axis=0).astype(bf16)


def dft_rows(channels, width):
    shape = (2 * len(channels), GROUP * width)
    row = lax.broadcasted_iota(jnp.int32, shape, 0)
    lane = lax.broadcasted_iota(jnp.int32, shape, 1)
    channel = jnp.zeros(shape, jnp.int32)
    for index, one in enumerate(channels):
        channel = jnp.where(row // 2 == index, one, channel)
    angle = lax.rem(channel * lax.rem(lane, width), width).astype(f32) * (full_turn / width)
    values = jnp.where(row % 2 == 0, jnp.cos(angle), -jnp.sin(angle))
    shape = (GROUP, GROUP * width)
    own = lax.broadcasted_iota(jnp.int32, shape, 1) // width == lax.broadcasted_iota(jnp.int32, shape, 0)
    spread = [jnp.where(own, jnp.broadcast_to(values[i : i + 1], shape), 0.0) for i in range(2 * len(channels))]
    return jnp.concatenate(spread, axis=0)


def steering(me, order, positions, beam_dirs, channel, channels):
    owners = len(order)
    stations = positions.shape[1] // owners
    columns = jnp.concatenate([positions, jnp.zeros((6, positions.shape[1]), f32)], axis=0).T
    span = 1
    while span < owners:
        parts = [columns[i * stations : (i + 1) * stations] for i in range(owners)]
        turned = jnp.concatenate([parts[i ^ span] for i in range(owners)], axis=0)
        columns = jnp.where((me & span) != 0, turned, columns)
        span *= 2
    columns = jnp.concatenate([columns[d * stations : (d + 1) * stations] for d in order], axis=0)
    bearing = beam_dirs.astype(f32) * (full_turn / DIRS)
    frequency = 1.0 + channel.astype(f32) / channels
    path_delay = columns[:, 0:1] * jnp.cos(bearing) + columns[:, 1:2] * jnp.sin(bearing)
    turns = frequency * path_delay
    phases = full_turn * (turns - jnp.round(turns))
    return jnp.concatenate([jnp.cos(phases), jnp.sin(phases)], axis=0)


def channelize_kernel(owners, slots, part, order, places, joined, other_count, *refs):
    count = owners * slots
    has_halo = part != "second"
    chans_in, volts, taps_in = refs[:3]
    others = refs[3 + 3 * has_halo : 3 + 3 * has_halo + other_count]
    outs = refs[3 + 3 * has_halo + other_count : len(refs) - 10]
    dft, held, high, low, chans, taps, sems, chans_sem, taps_sem, halo_sem = refs[-10:]
    stations, width, snaps = volts.shape
    chunk = held.shape[2] - LANES
    tap_count = taps.shape[0]
    step = tap_count // 2
    rows = 2 * GROUP
    half = count * rows
    pieces = sems.shape[0]
    piece = stations // pieces
    small = [pltpu.make_async_copy(chans_in, chans, chans_sem), pltpu.make_async_copy(taps_in, taps, taps_sem)]
    if has_halo:
        small.append(pltpu.make_async_copy(refs[3], held.at[:, :, :LANES], halo_sem))
    copies = []
    for index in range(pieces):
        members = pl.ds(index * piece, piece)
        if has_halo:
            source, target = volts.at[members, :, :chunk], held.at[members, :, LANES:]
        else:
            source, target = volts.at[members, :, snaps - chunk - LANES :], held.at[members]
        copies.append(pltpu.make_async_copy(source, target, sems.at[index]))
    for copy in small + copies:
        copy.start()
    for copy in small:
        copy.wait()

    me = lax.axis_index("stn")
    table = dft_rows([chans[(me ^ d) * slots + slot] for slot in range(slots) for d in range(owners)], width)
    dft[:half], dft[half:] = split_in_two(table)
    columns = taps[...].T
    tap = [jnp.broadcast_to(columns[:, m : m + 1], (width, chunk + LANES)) for m in range(tap_count)]
    results = []
    for station in range(stations):
        if station % piece == 0:
            copies[station // piece].wait()
        now = held[station]
        shifted = [(pltpu.roll(now, m, axis=1) if m else now).astype(f32) for m in range(step)]
        near = sum(tap[m] * shifted[m] for m in range(step))
        far = sum(tap[step + m] * shifted[m] for m in range(step))
        filtered = (near + pltpu.roll(far, step, axis=1))[:, LANES:]
        member = station % GROUP
        high[pl.ds(member * width, width), :], low[pl.ds(member * width, width), :] = split_in_two(filtered)
        if member == GROUP - 1:
            both = jnp.dot(dft[...], high[...], preferred_element_type=f32)
            cross = jnp.dot(dft[:half], low[...], preferred_element_type=f32)
            results.append(both[:half] + (both[half:] + cross))
    for index in range(count):
        slot, d = divmod(index, owners)
        number, entry = places[slot, d]
        target = outs[number].at[entry]
        for real in range(2):
            first = index * rows + real * GROUP
            merged = jnp.concatenate([one[first : first + GROUP] for one in results], axis=0)
            target[real, :, :chunk] = merged.astype(bf16)
        if (slot, d) in joined:
            at, inside = joined[slot, d]
            target[:, :, chunk:] = others[at][inside]
    if not has_halo:
        outs[-1][...] = held[:, :, chunk:]
    else:
        for slot in range(slots):
            channel = chans[me * slots + slot]
            outs[-1][slot] = steering(me, order, refs[4][...], refs[5][...], channel, owners * slots)


def channelize(slots, part, order, layout, chans, volts, taps, halo=None, positions=None, beam_dirs=None, joined=None):
    stations, width, snaps = volts.shape
    owners = len(order)
    count = owners * slots
    chunk = snaps // 2
    pieces = max(stations // 4, 1)
    joined = joined or {}
    others = []
    for array, _ in joined.values():
        if not any(array is one for one in others):
            others.append(array)
    number_of = lambda array: next(i for i, one in enumerate(others) if one is array)
    joined = {key: (number_of(array), entry) for key, (array, entry) in joined.items()}
    places, out_shape = {}, []
    for number, keys in enumerate(layout):
        for entry, key in enumerate(keys):
            places[key] = (number, entry)
        length = snaps if keys[0] in joined else chunk
        out_shape.append(jax.ShapeDtypeStruct((len(keys), 2, stations, length), bf16))
    if halo is None:
        out_shape.append(jax.ShapeDtypeStruct((stations, width, LANES), bf16))
    else:
        out_shape.append(jax.ShapeDtypeStruct((slots, 2 * owners * stations, beam_dirs.shape[0]), f32))
    operands = [pltpu.with_memory_space_constraint(one, pltpu.HBM) for one in (chans, volts, taps)]
    operands += ([] if halo is None else [halo, positions, beam_dirs[None, :]]) + others
    return pl.pallas_call(
        functools.partial(channelize_kernel, owners, slots, part, order, places, joined, len(others)),
        in_specs=[pl.BlockSpec(memory_space=pltpu.HBM)] * 3
        + [pl.BlockSpec(memory_space=pl.ANY)] * (halo is not None)
        + [pl.BlockSpec(memory_space=pltpu.VMEM)] * (len(operands) - 3 - (halo is not None)),
        out_specs=[pl.BlockSpec(memory_space=pltpu.VMEM)] * len(out_shape),
        out_shape=out_shape,
        scratch_shapes=[
            pltpu.VMEM((4 * count * GROUP, GROUP * width), bf16),
            pltpu.VMEM((stations, width, chunk + LANES), bf16),
            pltpu.VMEM((GROUP * width, chunk), bf16),
            pltpu.VMEM((GROUP * width, chunk), bf16),
            pltpu.SMEM(chans.shape, jnp.int32),
            pltpu.VMEM(taps.shape, f32),
            pltpu.SemaphoreType.DMA((pieces,)),
            pltpu.SemaphoreType.DMA(()),
            pltpu.SemaphoreType.DMA(()),
            pltpu.SemaphoreType.DMA(()),
        ],
        compiler_params=pltpu.CompilerParams(vmem_limit_bytes=VMEM_BYTES),
        cost_estimate=QUICK,
        name="channelize_" + part,
    )(*operands)


def flattened(blocks):
    arrays, numbered = [], []
    for block in blocks:
        numbered.append([])
        for array, entry in block:
            found = [i for i, one in enumerate(arrays) if one is array]
            if not found:
                found = [len(arrays)]
                arrays.append(array)
            numbered[-1].append((found[0], entry))
    return arrays, numbered


def stacked_rows(blocks, refs):
    rows = []
    for part in range(2):
        for block in blocks:
            rows.append(jnp.concatenate([refs[at][entry, part] for at, entry in block], axis=1))
    return merged_rows(rows)


def first_gram_kernel(blocks, *refs):
    out = refs[-1]
    slots, half, wide = out.shape
    row = lax.broadcasted_iota(jnp.int32, (half, half), 0)
    column = lax.broadcasted_iota(jnp.int32, (half, half), 1)
    for slot in range(slots):
        stacked = stacked_rows(blocks[slot], refs[:-1])
        gram = lax.dot_general(stacked, stacked, NT, preferred_element_type=f32)
        sym_part = gram[:half, :half] + gram[half:, half:]
        skew_part = gram[half:, :half] - gram[:half, half:]
        packed = jnp.where(row >= column, sym_part, skew_part)
        out[slot] = jnp.concatenate([packed, jnp.zeros((half, wide - half), f32)], axis=1)


def last_gram_kernel(blocks, count, *refs):
    out = refs[-1]
    slots, double, half = out.shape
    rows = double // 2
    for slot in range(slots):
        stacked = stacked_rows(blocks[slot], refs[:-1])
        ours = stacked_rows(blocks[slot][-count:], refs[:-1])
        gram = lax.dot_general(ours, stacked, NT, preferred_element_type=f32)
        out[slot, :rows] = gram[:rows, :half] + gram[rows:, half:]
        out[slot, rows:] = gram[rows:, :half] - gram[:rows, half:]


def gram_call(kernel, blocks, shape, name):
    operands, numbered = flattened([block for one in blocks for block in one])
    per_slot = len(blocks[0])
    numbered = [numbered[i * per_slot : (i + 1) * per_slot] for i in range(len(blocks))]
    return pl.pallas_call(
        functools.partial(kernel, numbered),
        in_specs=[pl.BlockSpec(memory_space=pltpu.VMEM)] * len(operands),
        out_specs=pl.BlockSpec(memory_space=pltpu.VMEM),
        out_shape=jax.ShapeDtypeStruct((len(blocks), *shape), f32),
        compiler_params=pltpu.CompilerParams(vmem_limit_bytes=GRAM_VMEM),
        cost_estimate=QUICK,
        name=name,
    )(*operands)


def first_gram(blocks, stations, half):
    return gram_call(first_gram_kernel, blocks, (stations, half), "first_gram")


def last_gram(blocks, count, stations, half):
    kernel = lambda numbered, *refs: last_gram_kernel(numbered, count, *refs)
    return gram_call(kernel, blocks, (2 * stations, half), "last_gram")


def dot(left, right, dims=NN):
    return lax.dot_general(left, right, dims, precision=lax.Precision.HIGHEST, preferred_element_type=f32)


def split_in_three(value):
    high, rest = value.astype(bf16), value
    rest = rest - high.astype(f32)
    middle = rest.astype(bf16)
    return high, middle, (rest - middle.astype(f32)).astype(bf16)


def deep_dot(left, right):
    a, b = split_in_three(left), split_in_three(right)
    left = jnp.concatenate([a[0], a[0], a[1], a[1], a[0], a[2]], axis=0)
    right = jnp.concatenate([b[0], b[1], b[0], b[1], b[2], b[0]], axis=0)
    return lax.dot_general(left, right, TN, preferred_element_type=f32)


def sweep_rows(systems, lanes, at_once):
    count, width = systems[0][0].shape
    narrow = (count, LANES)
    index, index_wide = (lax.broadcasted_iota(jnp.int32, shape, 0) for shape in (narrow, (count, width)))
    repeated = lambda value: jnp.concatenate([value] * (width // LANES), axis=1)
    rows = list(systems)
    for start in range(0, count, at_once):
        fetched = lanes[start : start + at_once]
        columns = [
            [tuple(jnp.broadcast_to(part[:, lane : lane + 1], narrow) for part in row) for lane in fetched] for row in rows
        ]
        for j in range(len(fetched)):
            step = start + j
            spread = lambda value: jnp.broadcast_to(value[step : step + 1], value.shape)

            def swept(value, here, a, b, scale):
                real, imag = value
                pick_r, pick_i = spread(real) * scale, spread(imag) * scale
                return (
                    jnp.where(here, pick_r, real - (a * pick_r - b * pick_i)),
                    jnp.where(here, pick_i, imag - (a * pick_i + b * pick_r)),
                )

            scales = [1.0 / spread(column[j][0]) for column in columns]
            for later in range(j + 1, len(fetched)):
                for column, scale in zip(columns, scales):
                    column[later] = swept(column[later], index == step, *column[j], scale)
            for number, (column, scale) in enumerate(zip(columns, scales)):
                a, b = column[j]
                rows[number] = swept(rows[number], index_wide == step, repeated(a), repeated(b), repeated(scale))
    return rows


def eliminate(systems, start, stop, pivots, at_once):
    half = systems[0][0].shape[0]
    shape = systems[0][0].shape
    rank = lax.broadcasted_iota(jnp.int32, shape, 0)
    lane = lax.broadcasted_iota(jnp.int32, shape, 1)
    for first in range(start, stop, pivots):
        last = first + pivots
        tile = first // LANES * LANES
        inside = (lane[first:last] >= first) & (lane[first:last] < last)
        minus_one = jnp.where(rank[first:last] == lane[first:last], -1.0, 0.0)
        sides, rows = [], []
        for real, imag in systems:
            row_r, row_i = real[first:last], imag[first:last]
            upper = jnp.concatenate([row_r[:, :half], -row_i[:, :half]], axis=1)
            lower = jnp.concatenate([row_i[:, :half], row_r[:, :half]], axis=1)
            sides.append(jnp.concatenate([upper, lower], axis=0))
            rows.append((
                jnp.concatenate([row_r[:, tile : tile + LANES], jnp.where(inside, minus_one, row_r)], axis=1),
                jnp.concatenate([row_i[:, tile : tile + LANES], jnp.where(inside, 0.0, row_i)], axis=1),
            ))
        rows = sweep_rows(rows, range(first - tile, last - tile), at_once)
        own = (rank >= first) & (rank < last)
        gone = (lane >= first) & (lane < last)
        spread = lambda piece: jnp.concatenate([piece] * (half // pivots), axis=0)
        results = []
        for (real, imag), side, (row_r, row_i) in zip(systems, sides, rows):
            row_r, row_i = row_r[:, LANES:], row_i[:, LANES:]
            update = deep_dot(side, jnp.concatenate([row_r, row_i], axis=0))
            results.append((
                jnp.where(own, spread(row_r), jnp.where(gone, 0.0, real) - update[:half]),
                jnp.where(own, spread(row_i), jnp.where(gone, 0.0, imag) - update[half:]),
            ))
        systems = results
    return systems


def first_solve_kernel(segments, snap_total, *refs):
    grams, steer, out = refs[:segments], refs[segments], refs[-1]
    slots, stations, half = grams[0].shape
    row = lax.broadcasted_iota(jnp.int32, (half, half), 0)
    column = lax.broadcasted_iota(jnp.int32, (half, half), 1)
    systems = []
    for slot in range(slots):
        packed = sum(one[slot] for one in grams) * (1.0 / snap_total)
        if stations < half:
            packed = jnp.concatenate([packed, jnp.zeros((half - stations, half), f32)], axis=0)
        turned = packed.T
        real = jnp.where(row >= column, packed, turned)
        real = jnp.where((row == column) & (row < stations), real + loading_level, real)
        imag = jnp.where(row < column, packed, jnp.where(row > column, -turned, 0.0))
        known = row < stations
        systems.append((
            jnp.concatenate([real, jnp.where(known, steer[slot, :half], 0.0)], axis=1),
            jnp.concatenate([imag, jnp.where(known, steer[slot, half:], 0.0)], axis=1),
        ))
    for slot, (real, imag) in enumerate(eliminate(systems, 0, stations, math.gcd(stations, PIVOTS), AT_ONCE)):
        out[slot, 0] = jnp.concatenate([real, systems[slot][0][:, :half]], axis=1)
        out[slot, 1] = jnp.concatenate([imag, systems[slot][1][:, :half]], axis=1)


def first_solve(snap_total, grams, steer):
    slots, _, count = steer.shape
    half = grams[0].shape[2]
    return pl.pallas_call(
        functools.partial(first_solve_kernel, len(grams), snap_total),
        in_specs=[pl.BlockSpec(memory_space=pltpu.VMEM)] * (len(grams) + 1),
        out_specs=pl.BlockSpec(memory_space=pltpu.VMEM),
        out_shape=jax.ShapeDtypeStruct((slots, 2, half, 2 * half + count), f32),
        compiler_params=pltpu.CompilerParams(vmem_limit_bytes=BEAMS_VMEM),
        cost_estimate=QUICK,
        name="first_solve",
    )(*grams, steer)


def complex_rows(real, imag):
    upper = jnp.concatenate([real, -imag], axis=1)
    return jnp.concatenate([upper, jnp.concatenate([imag, real], axis=1)], axis=0)


def joined_system(swept_r, swept_i, rows_r, rows_i, steer_r, steer_i, known):
    count, half = rows_r.shape
    end = half + steer_r.shape[1]
    lane = lax.broadcasted_iota(jnp.int32, rows_r.shape, 1)
    cross_r, cross_i = jnp.where(lane < known, rows_r, 0.0), jnp.where(lane < known, rows_i, 0.0)
    stacked = lambda first, last: jnp.concatenate([swept_r[:, first:last], swept_i[:, first:last]], axis=0)
    inverse, matrix = stacked(0, half), stacked(end, end + half)
    guess = -dot(complex_rows(cross_r, cross_i), inverse)
    rest = jnp.concatenate([cross_r, cross_i], axis=0) - dot(complex_rows(guess[:count], guess[count:]), matrix)
    guess = guess - dot(complex_rows(rest[:count], rest[count:]), inverse)
    turn_r, turn_i = guess[:count], guess[count:]
    ahead = lax.broadcasted_iota(jnp.int32, steer_r.shape, 0) < known
    first_steer = jnp.concatenate([jnp.where(ahead, steer_r, 0.0), jnp.where(ahead, steer_i, 0.0)], axis=0)
    taken = dot(complex_rows(turn_r, turn_i), first_steer)
    back_r, back_i = steer_r[known:] - taken[:count], steer_i[known:] - taken[count:]
    left = jnp.concatenate(
        [jnp.concatenate([turn_r, turn_i], axis=1), jnp.concatenate([turn_i, -turn_r], axis=1)], axis=0
    )
    right = jnp.concatenate([jnp.zeros((known, 2 * half), f32), jnp.concatenate([cross_r, cross_i], axis=1)], axis=0)
    inner = dot(left, right, NT)
    rows_r = jnp.where(lane < known, turn_r, rows_r - inner[:count])
    rows_i = jnp.where(lane < known, turn_i, rows_i - inner[count:])
    real = jnp.concatenate([swept_r[:known, :end], jnp.concatenate([rows_r, back_r], axis=1)], axis=0)
    imag = jnp.concatenate([swept_i[:known, :end], jnp.concatenate([rows_i, back_i], axis=1)], axis=0)
    return real, imag


def beams_kernel(segments, snap_total, blocks, *refs):
    grams, swept, steer = refs[:segments], refs[segments], refs[segments + 1]
    arrays, out, mix = refs[segments + 2 : -2], refs[-2], refs[-1]
    slots, double, half = grams[0].shape
    known = half - double // 2
    count = steer.shape[2]

    @pl.when(pl.program_id(0) == 0)
    def _():
        systems = []
        shape = (double // 2, half)
        diagonal = lax.broadcasted_iota(jnp.int32, shape, 0) + known == lax.broadcasted_iota(jnp.int32, shape, 1)
        for slot in range(slots):
            rows = sum(one[slot] for one in grams) * (1.0 / snap_total)
            rows_r, rows_i = rows[: double // 2], rows[double // 2 :]
            rows_r = jnp.where(diagonal, rows_r + loading_level, rows_r)
            steer_r, steer_i = steer[slot, :half], steer[slot, half:]
            systems.append(joined_system(swept[slot, 0], swept[slot, 1], rows_r, rows_i, steer_r, steer_i, known))
        for slot, (real, imag) in enumerate(eliminate(systems, known, half, math.gcd(known, PIVOTS), AT_ONCE)):
            solved_r, solved_i = real[:, half:], imag[:, half:]
            power = jnp.sum(steer[slot, :half] * solved_r + steer[slot, half:] * solved_i, axis=0, keepdims=True)
            scale = 1.0 / jnp.sqrt(power)
            weight_r, weight_i = (solved_r * scale).T, (solved_i * scale).T
            mix[slot, :count] = jnp.concatenate([weight_r, weight_i], axis=1).astype(bf16)
            mix[slot, count:] = jnp.concatenate([-weight_i, weight_r], axis=1).astype(bf16)

    for slot in range(slots):

        @pl.when(pl.program_id(0) == slot)
        def _():
            mixed = jnp.dot(mix[slot], stacked_rows(blocks[slot], arrays), preferred_element_type=f32).astype(bf16)
            out[0, 0] = mixed[:count]
            out[0, 1] = mixed[count:]


def beams(snap_total, grams, swept, steer, blocks):
    slots, double, count = steer.shape
    arrays, numbered = flattened([block for one in blocks for block in one])
    per_slot = len(blocks[0])
    numbered = [numbered[i * per_slot : (i + 1) * per_slot] for i in range(slots)]
    snaps = sum(array.shape[-1] for array, _ in blocks[0][0])
    operands = [*grams, swept, steer, *arrays]
    return pl.pallas_call(
        functools.partial(beams_kernel, len(grams), snap_total, numbered),
        grid=(slots,),
        in_specs=[pl.BlockSpec(memory_space=pltpu.VMEM)] * len(operands),
        out_specs=pl.BlockSpec((1, 2, count, snaps), lambda i: (i, 0, 0, 0)),
        out_shape=jax.ShapeDtypeStruct((slots, 2, count, snaps), bf16),
        scratch_shapes=[pltpu.VMEM((slots, 2 * count, double), bf16)],
        compiler_params=pltpu.CompilerParams(vmem_limit_bytes=BEAMS_VMEM),
        cost_estimate=QUICK,
        name="beams",
    )(*operands)


def partners(value, axis, distance):
    length = lax.axis_size(axis)
    return lax.ppermute(value, axis, [(i, i ^ distance) for i in range(length)])


def segment_sums(packed):
    length = lax.axis_size("seg")
    if length <= 4:
        return [packed] + [partners(packed, "seg", d) for d in range(1, length)]
    distance = 1
    while distance < length:
        packed = packed + partners(packed, "seg", distance)
        distance *= 2
    return [packed]


def after(value, *earlier):
    return lax.optimization_barrier((value, *earlier))


def on_device(voltages, filter_taps, positions, beam_dirs, chan_table):
    stations, width, snaps = voltages.shape
    channels = chan_table.shape[0]
    owners = lax.axis_size("stn")
    segments = lax.axis_size("seg")
    slots = channels // owners
    half = owners * stations
    snap_total = snaps * segments
    near, far = list(range(1, owners // 2)), list(range(owners // 2, owners))
    split, unsplit = far[: len(far) // 2], far[len(far) // 2 :]
    late_ones = near[-1:] + unsplit if len(near) > 1 else unsplit
    order = [d for d in range(owners) if d not in late_ones] + late_ones
    known = (owners - len(late_ones)) * stations
    together = lambda d: [[(slot, d) for slot in range(slots)]]
    apart = lambda d: [[(slot, d)] for slot in range(slots)]
    middle = [d for d in near if d not in late_ones and d > 1]
    sent = [keys for d in split for keys in together(d)] + [keys for d in middle for keys in apart(d)] + together(1)
    outer = [keys for d in late_ones for keys in together(d)]
    layout = sent + outer + together(0)
    *second, last = channelize(slots, "second", order, layout, chan_table, voltages, filter_taps)
    late = [partners(one, "stn", d) for d, one in zip(split, second)]
    halo = lax.ppermute(last, "seg", [(i, i + 1) for i in range(segments - 1)])
    joined = {key: (one, i) for keys, one in zip(layout[len(split) :], second[len(split) :]) for i, key in enumerate(keys)}
    *first, steer = channelize(
        slots, "first", order, layout, chan_table, voltages, filter_taps, halo, positions, beam_dirs, joined
    )
    first, steer, late = after(first, steer, late)
    early = [partners(one, "stn", keys[0][1]) for one, keys in zip(first, sent)]
    following, early[: len(split)] = after(first[len(sent) : -1], early[: len(split)])
    following = [partners(one, "stn", keys[0][1]) for one, keys in zip(following, outer)]
    held = {}
    for keys, one in zip(layout, early + following + first[-1:]):
        held.update({key: [(one, i)] for i, key in enumerate(keys)})
    for keys, one in zip(layout, late):
        for i, key in enumerate(keys):
            held[key].append((one, i))
    blocks = lambda ds: [[held[slot, d] for d in ds] for slot in range(slots)]
    grams = segment_sums(first_gram(blocks([d for d in order if d not in late_ones]), known, half))
    swept = first_solve(snap_total, grams, steer)
    following, swept = after(following, swept)
    for keys, one in zip(outer, following):
        held.update({key: [(one, i)] for i, key in enumerate(keys)})
    grams = segment_sums(last_gram(blocks(order), len(late_ones), half - known, half))
    return beams(snap_total, grams, swept, steer, blocks(order))


def solution(mesh):
    return jax.shard_map(
        on_device,
        mesh=mesh,
        in_specs=(P("stn", None, "seg"), P(), P(), P(), P()),
        out_specs=P("stn", None, None, "seg"),
        check_vma=False,
    )
```

```python
import functools
import math

import jax
import jax.numpy as jnp
from jax import lax
from jax.experimental import pallas as pl
from jax.experimental.pallas import tpu as pltpu
from jax.sharding import PartitionSpec as P

DIRS = 360
LANES = 128
GROUP = 8
PIVOTS = 16
QUICK = pl.CostEstimate(flops=1000, bytes_accessed=1000, transcendentals=0)
AT_ONCE = 4
VMEM_BYTES = 16 << 20
GRAM_VMEM = 8 << 20
BEAMS_VMEM = 12 << 20

loading_level = 0.1
full_turn = 2.0 * math.pi
NN = (((1,), (0,)), ((), ()))
NT = (((1,), (1,)), ((), ()))
TN = (((0,), (0,)), ((), ()))
f32, bf16 = jnp.float32, jnp.bfloat16


def split_in_two(value):
    high = value.astype(bf16)
    return high, (value - high.astype(f32)).astype(bf16)


def merged_rows(pieces):
    if all(piece.shape[0] % 16 == 0 for piece in pieces):
        return jnp.concatenate(pieces, axis=0)
    return jnp.concatenate([piece.astype(f32) for piece in pieces], axis=0).astype(bf16)


def dft_rows(channels, width):
    shape = (2 * len(channels), GROUP * width)
    row = lax.broadcasted_iota(jnp.int32, shape, 0)
    lane = lax.broadcasted_iota(jnp.int32, shape, 1)
    channel = jnp.zeros(shape, jnp.int32)
    for index, one in enumerate(channels):
        channel = jnp.where(row // 2 == index, one, channel)
    angle = lax.rem(channel * lax.rem(lane, width), width).astype(f32) * (full_turn / width)
    values = jnp.where(row % 2 == 0, jnp.cos(angle), -jnp.sin(angle))
    shape = (GROUP, GROUP * width)
    own = lax.broadcasted_iota(jnp.int32, shape, 1) // width == lax.broadcasted_iota(jnp.int32, shape, 0)
    spread = [jnp.where(own, jnp.broadcast_to(values[i : i + 1], shape), 0.0) for i in range(2 * len(channels))]
    return jnp.concatenate(spread, axis=0)


def steering(me, order, positions, beam_dirs, channel, channels):
    owners = len(order)
    stations = positions.shape[1] // owners
    columns = jnp.concatenate([positions, jnp.zeros((6, positions.shape[1]), f32)], axis=0).T
    span = 1
    while span < owners:
        parts = [columns[i * stations : (i + 1) * stations] for i in range(owners)]
        turned = jnp.concatenate([parts[i ^ span] for i in range(owners)], axis=0)
        columns = jnp.where((me & span) != 0, turned, columns)
        span *= 2
    columns = jnp.concatenate([columns[d * stations : (d + 1) * stations] for d in order], axis=0)
    bearing = beam_dirs.astype(f32) * (full_turn / DIRS)
    frequency = 1.0 + channel.astype(f32) / channels
    path_delay = columns[:, 0:1] * jnp.cos(bearing) + columns[:, 1:2] * jnp.sin(bearing)
    turns = frequency * path_delay
    phases = full_turn * (turns - jnp.round(turns))
    return jnp.concatenate([jnp.cos(phases), jnp.sin(phases)], axis=0)


def channelize_kernel(owners, slots, part, order, places, joined, other_count, *refs):
    count = owners * slots
    has_halo = part != "second"
    chans_in, volts, taps_in = refs[:3]
    others = refs[3 + 3 * has_halo : 3 + 3 * has_halo + other_count]
    outs = refs[3 + 3 * has_halo + other_count : len(refs) - 10]
    dft, held, high, low, chans, taps, sems, chans_sem, taps_sem, halo_sem = refs[-10:]
    stations, width, snaps = volts.shape
    chunk = held.shape[2] - LANES
    tap_count = taps.shape[0]
    step = tap_count // 2
    rows = 2 * GROUP
    half = count * rows
    pieces = sems.shape[0]
    piece = stations // pieces
    small = [pltpu.make_async_copy(chans_in, chans, chans_sem), pltpu.make_async_copy(taps_in, taps, taps_sem)]
    if has_halo:
        small.append(pltpu.make_async_copy(refs[3], held.at[:, :, :LANES], halo_sem))
    copies = []
    for index in range(pieces):
        members = pl.ds(index * piece, piece)
        if has_halo:
            source, target = volts.at[members, :, :chunk], held.at[members, :, LANES:]
        else:
            source, target = volts.at[members, :, snaps - chunk - LANES :], held.at[members]
        copies.append(pltpu.make_async_copy(source, target, sems.at[index]))
    for copy in small + copies:
        copy.start()
    for copy in small:
        copy.wait()

    me = lax.axis_index("stn")
    table = dft_rows([chans[(me ^ d) * slots + slot] for slot in range(slots) for d in range(owners)], width)
    dft[:half], dft[half:] = split_in_two(table)
    columns = taps[...].T
    tap = [jnp.broadcast_to(columns[:, m : m + 1], (width, chunk + LANES)) for m in range(tap_count)]
    results = []
    for station in range(stations):
        if station % piece == 0:
            copies[station // piece].wait()
        now = held[station]
        shifted = [(pltpu.roll(now, m, axis=1) if m else now).astype(f32) for m in range(step)]
        near = sum(tap[m] * shifted[m] for m in range(step))
        far = sum(tap[step + m] * shifted[m] for m in range(step))
        filtered = (near + pltpu.roll(far, step, axis=1))[:, LANES:]
        member = station % GROUP
        high[pl.ds(member * width, width), :], low[pl.ds(member * width, width), :] = split_in_two(filtered)
        if member == GROUP - 1:
            both = jnp.dot(dft[...], high[...], preferred_element_type=f32)
            cross = jnp.dot(dft[:half], low[...], preferred_element_type=f32)
            results.append(both[:half] + (both[half:] + cross))
    for index in range(count):
        slot, d = divmod(index, owners)
        number, entry = places[slot, d]
        target = outs[number].at[entry]
        for real in range(2):
            first = index * rows + real * GROUP
            merged = jnp.concatenate([one[first : first + GROUP] for one in results], axis=0)
            target[real, :, :chunk] = merged.astype(bf16)
        if (slot, d) in joined:
            at, inside = joined[slot, d]
            target[:, :, chunk:] = others[at][inside]
    if has_halo:
        for slot in range(slots):
            channel = chans[me * slots + slot]
            outs[-1][slot] = steering(me, order, refs[4][...], refs[5][...], channel, owners * slots)


def channelize(slots, part, order, layout, chans, volts, taps, halo=None, positions=None, beam_dirs=None, joined=None):
    stations, width, snaps = volts.shape
    owners = len(order)
    count = owners * slots
    chunk = snaps // 2
    pieces = max(stations // 4, 1)
    joined = joined or {}
    others = []
    for array, _ in joined.values():
        if not any(array is one for one in others):
            others.append(array)
    number_of = lambda array: next(i for i, one in enumerate(others) if one is array)
    joined = {key: (number_of(array), entry) for key, (array, entry) in joined.items()}
    places, out_shape = {}, []
    for number, keys in enumerate(layout):
        for entry, key in enumerate(keys):
            places[key] = (number, entry)
        length = snaps if keys[0] in joined else chunk
        out_shape.append(jax.ShapeDtypeStruct((len(keys), 2, stations, length), bf16))
    if halo is not None:
        out_shape.append(jax.ShapeDtypeStruct((slots, 2 * owners * stations, beam_dirs.shape[0]), f32))
    operands = [pltpu.with_memory_space_constraint(one, pltpu.HBM) for one in (chans, volts, taps)]
    operands += ([] if halo is None else [halo, positions, beam_dirs[None, :]]) + others
    return pl.pallas_call(
        functools.partial(channelize_kernel, owners, slots, part, order, places, joined, len(others)),
        in_specs=[pl.BlockSpec(memory_space=pltpu.HBM)] * 3
        + [pl.BlockSpec(memory_space=pl.ANY)] * (halo is not None)
        + [pl.BlockSpec(memory_space=pltpu.VMEM)] * (len(operands) - 3 - (halo is not None)),
        out_specs=[pl.BlockSpec(memory_space=pltpu.VMEM)] * len(out_shape),
        out_shape=out_shape,
        scratch_shapes=[
            pltpu.VMEM((4 * count * GROUP, GROUP * width), bf16),
            pltpu.VMEM((stations, width, chunk + LANES), bf16),
            pltpu.VMEM((GROUP * width, chunk), bf16),
            pltpu.VMEM((GROUP * width, chunk), bf16),
            pltpu.SMEM(chans.shape, jnp.int32),
            pltpu.VMEM(taps.shape, f32),
            pltpu.SemaphoreType.DMA((pieces,)),
            pltpu.SemaphoreType.DMA(()),
            pltpu.SemaphoreType.DMA(()),
            pltpu.SemaphoreType.DMA(()),
        ],
        compiler_params=pltpu.CompilerParams(vmem_limit_bytes=VMEM_BYTES),
        cost_estimate=QUICK,
        name="channelize_" + part,
    )(*operands)


def flattened(blocks):
    arrays, numbered = [], []
    for block in blocks:
        numbered.append([])
        for array, entry in block:
            found = [i for i, one in enumerate(arrays) if one is array]
            if not found:
                found = [len(arrays)]
                arrays.append(array)
            numbered[-1].append((found[0], entry))
    return arrays, numbered


def stacked_rows(blocks, refs):
    rows = []
    for part in range(2):
        for block in blocks:
            rows.append(jnp.concatenate([refs[at][entry, part] for at, entry in block], axis=1))
    return merged_rows(rows)


def first_gram_kernel(blocks, *refs):
    out = refs[-1]
    slots, half, wide = out.shape
    row = lax.broadcasted_iota(jnp.int32, (half, half), 0)
    column = lax.broadcasted_iota(jnp.int32, (half, half), 1)
    for slot in range(slots):
        stacked = stacked_rows(blocks[slot], refs[:-1])
        gram = lax.dot_general(stacked, stacked, NT, preferred_element_type=f32)
        sym_part = gram[:half, :half] + gram[half:, half:]
        skew_part = gram[half:, :half] - gram[:half, half:]
        packed = jnp.where(row >= column, sym_part, skew_part)
        out[slot] = jnp.concatenate([packed, jnp.zeros((half, wide - half), f32)], axis=1)


def last_gram_kernel(blocks, count, *refs):
    out = refs[-1]
    slots, double, half = out.shape
    rows = double // 2
    for slot in range(slots):
        stacked = stacked_rows(blocks[slot], refs[:-1])
        ours = stacked_rows(blocks[slot][-count:], refs[:-1])
        gram = lax.dot_general(ours, stacked, NT, preferred_element_type=f32)
        out[slot, :rows] = gram[:rows, :half] + gram[rows:, half:]
        out[slot, rows:] = gram[rows:, :half] - gram[:rows, half:]


def gram_call(kernel, blocks, shape, name):
    operands, numbered = flattened([block for one in blocks for block in one])
    per_slot = len(blocks[0])
    numbered = [numbered[i * per_slot : (i + 1) * per_slot] for i in range(len(blocks))]
    return pl.pallas_call(
        functools.partial(kernel, numbered),
        in_specs=[pl.BlockSpec(memory_space=pltpu.VMEM)] * len(operands),
        out_specs=pl.BlockSpec(memory_space=pltpu.VMEM),
        out_shape=jax.ShapeDtypeStruct((len(blocks), *shape), f32),
        compiler_params=pltpu.CompilerParams(vmem_limit_bytes=GRAM_VMEM),
        cost_estimate=QUICK,
        name=name,
    )(*operands)


def first_gram(blocks, stations, half):
    return gram_call(first_gram_kernel, blocks, (stations, half), "first_gram")


def last_gram(blocks, count, stations, half):
    kernel = lambda numbered, *refs: last_gram_kernel(numbered, count, *refs)
    return gram_call(kernel, blocks, (2 * stations, half), "last_gram")


def dot(left, right, dims=NN):
    return lax.dot_general(left, right, dims, precision=lax.Precision.HIGHEST, preferred_element_type=f32)


def split_in_three(value):
    high, rest = value.astype(bf16), value
    rest = rest - high.astype(f32)
    middle = rest.astype(bf16)
    return high, middle, (rest - middle.astype(f32)).astype(bf16)


def deep_dot(left, right):
    a, b = split_in_three(left), split_in_three(right)
    left = jnp.concatenate([a[0], a[0], a[1], a[1], a[0], a[2]], axis=0)
    right = jnp.concatenate([b[0], b[1], b[0], b[1], b[2], b[0]], axis=0)
    return lax.dot_general(left, right, TN, preferred_element_type=f32)


def sweep_rows(systems, lanes, at_once):
    count, width = systems[0][0].shape
    narrow = (count, LANES)
    index, index_wide = (lax.broadcasted_iota(jnp.int32, shape, 0) for shape in (narrow, (count, width)))
    repeated = lambda value: jnp.concatenate([value] * (width // LANES), axis=1)
    rows = list(systems)
    for start in range(0, count, at_once):
        fetched = lanes[start : start + at_once]
        columns = [
            [tuple(jnp.broadcast_to(part[:, lane : lane + 1], narrow) for part in row) for lane in fetched] for row in rows
        ]
        for j in range(len(fetched)):
            step = start + j
            spread = lambda value: jnp.broadcast_to(value[step : step + 1], value.shape)

            def swept(value, here, a, b, scale):
                real, imag = value
                pick_r, pick_i = spread(real) * scale, spread(imag) * scale
                return (
                    jnp.where(here, pick_r, real - (a * pick_r - b * pick_i)),
                    jnp.where(here, pick_i, imag - (a * pick_i + b * pick_r)),
                )

            scales = [1.0 / spread(column[j][0]) for column in columns]
            for later in range(j + 1, len(fetched)):
                for column, scale in zip(columns, scales):
                    column[later] = swept(column[later], index == step, *column[j], scale)
            for number, (column, scale) in enumerate(zip(columns, scales)):
                a, b = column[j]
                rows[number] = swept(rows[number], index_wide == step, repeated(a), repeated(b), repeated(scale))
    return rows


def eliminate(systems, start, stop, pivots, at_once):
    half = systems[0][0].shape[0]
    shape = systems[0][0].shape
    rank = lax.broadcasted_iota(jnp.int32, shape, 0)
    lane = lax.broadcasted_iota(jnp.int32, shape, 1)
    for first in range(start, stop, pivots):
        last = first + pivots
        tile = first // LANES * LANES
        inside = (lane[first:last] >= first) & (lane[first:last] < last)
        minus_one = jnp.where(rank[first:last] == lane[first:last], -1.0, 0.0)
        sides, rows = [], []
        for real, imag in systems:
            row_r, row_i = real[first:last], imag[first:last]
            upper = jnp.concatenate([row_r[:, :half], -row_i[:, :half]], axis=1)
            lower = jnp.concatenate([row_i[:, :half], row_r[:, :half]], axis=1)
            sides.append(jnp.concatenate([upper, lower], axis=0))
            rows.append((
                jnp.concatenate([row_r[:, tile : tile + LANES], jnp.where(inside, minus_one, row_r)], axis=1),
                jnp.concatenate([row_i[:, tile : tile + LANES], jnp.where(inside, 0.0, row_i)], axis=1),
            ))
        rows = sweep_rows(rows, range(first - tile, last - tile), at_once)
        own = (rank >= first) & (rank < last)
        gone = (lane >= first) & (lane < last)
        spread = lambda piece: jnp.concatenate([piece] * (half // pivots), axis=0)
        results = []
        for (real, imag), side, (row_r, row_i) in zip(systems, sides, rows):
            row_r, row_i = row_r[:, LANES:], row_i[:, LANES:]
            update = deep_dot(side, jnp.concatenate([row_r, row_i], axis=0))
            results.append((
                jnp.where(own, spread(row_r), jnp.where(gone, 0.0, real) - update[:half]),
                jnp.where(own, spread(row_i), jnp.where(gone, 0.0, imag) - update[half:]),
            ))
        systems = results
    return systems


def first_solve_kernel(segments, snap_total, *refs):
    grams, steer, out = refs[:segments], refs[segments], refs[-1]
    slots, stations, half = grams[0].shape
    row = lax.broadcasted_iota(jnp.int32, (half, half), 0)
    column = lax.broadcasted_iota(jnp.int32, (half, half), 1)
    systems = []
    for slot in range(slots):
        packed = sum(one[slot] for one in grams) * (1.0 / snap_total)
        if stations < half:
            packed = jnp.concatenate([packed, jnp.zeros((half - stations, half), f32)], axis=0)
        turned = packed.T
        real = jnp.where(row >= column, packed, turned)
        real = jnp.where((row == column) & (row < stations), real + loading_level, real)
        imag = jnp.where(row < column, packed, jnp.where(row > column, -turned, 0.0))
        known = row < stations
        systems.append((
            jnp.concatenate([real, jnp.where(known, steer[slot, :half], 0.0)], axis=1),
            jnp.concatenate([imag, jnp.where(known, steer[slot, half:], 0.0)], axis=1),
        ))
    for slot, (real, imag) in enumerate(eliminate(systems, 0, stations, math.gcd(stations, PIVOTS), AT_ONCE)):
        out[slot, 0] = jnp.concatenate([real, systems[slot][0][:, :half]], axis=1)
        out[slot, 1] = jnp.concatenate([imag, systems[slot][1][:, :half]], axis=1)


def first_solve(snap_total, grams, steer):
    slots, _, count = steer.shape
    half = grams[0].shape[2]
    return pl.pallas_call(
        functools.partial(first_solve_kernel, len(grams), snap_total),
        in_specs=[pl.BlockSpec(memory_space=pltpu.VMEM)] * (len(grams) + 1),
        out_specs=pl.BlockSpec(memory_space=pltpu.VMEM),
        out_shape=jax.ShapeDtypeStruct((slots, 2, half, 2 * half + count), f32),
        compiler_params=pltpu.CompilerParams(vmem_limit_bytes=BEAMS_VMEM),
        cost_estimate=QUICK,
        name="first_solve",
    )(*grams, steer)


def complex_rows(real, imag):
    upper = jnp.concatenate([real, -imag], axis=1)
    return jnp.concatenate([upper, jnp.concatenate([imag, real], axis=1)], axis=0)


def joined_system(swept_r, swept_i, rows_r, rows_i, steer_r, steer_i, known):
    count, half = rows_r.shape
    end = half + steer_r.shape[1]
    lane = lax.broadcasted_iota(jnp.int32, rows_r.shape, 1)
    cross_r, cross_i = jnp.where(lane < known, rows_r, 0.0), jnp.where(lane < known, rows_i, 0.0)
    stacked = lambda first, last: jnp.concatenate([swept_r[:, first:last], swept_i[:, first:last]], axis=0)
    inverse, matrix = stacked(0, half), stacked(end, end + half)
    guess = -dot(complex_rows(cross_r, cross_i), inverse)
    rest = jnp.concatenate([cross_r, cross_i], axis=0) - dot(complex_rows(guess[:count], guess[count:]), matrix)
    guess = guess - dot(complex_rows(rest[:count], rest[count:]), inverse)
    turn_r, turn_i = guess[:count], guess[count:]
    ahead = lax.broadcasted_iota(jnp.int32, steer_r.shape, 0) < known
    first_steer = jnp.concatenate([jnp.where(ahead, steer_r, 0.0), jnp.where(ahead, steer_i, 0.0)], axis=0)
    taken = dot(complex_rows(turn_r, turn_i), first_steer)
    back_r, back_i = steer_r[known:] - taken[:count], steer_i[known:] - taken[count:]
    left = jnp.concatenate(
        [jnp.concatenate([turn_r, turn_i], axis=1), jnp.concatenate([turn_i, -turn_r], axis=1)], axis=0
    )
    right = jnp.concatenate([jnp.zeros((known, 2 * half), f32), jnp.concatenate([cross_r, cross_i], axis=1)], axis=0)
    inner = dot(left, right, NT)
    rows_r = jnp.where(lane < known, turn_r, rows_r - inner[:count])
    rows_i = jnp.where(lane < known, turn_i, rows_i - inner[count:])
    real = jnp.concatenate([swept_r[:known, :end], jnp.concatenate([rows_r, back_r], axis=1)], axis=0)
    imag = jnp.concatenate([swept_i[:known, :end], jnp.concatenate([rows_i, back_i], axis=1)], axis=0)
    return real, imag


def beams_kernel(segments, snap_total, blocks, *refs):
    grams, swept, steer = refs[:segments], refs[segments], refs[segments + 1]
    arrays, out, mix = refs[segments + 2 : -2], refs[-2], refs[-1]
    slots, double, half = grams[0].shape
    known = half - double // 2
    count = steer.shape[2]

    @pl.when(pl.program_id(0) == 0)
    def _():
        systems = []
        shape = (double // 2, half)
        diagonal = lax.broadcasted_iota(jnp.int32, shape, 0) + known == lax.broadcasted_iota(jnp.int32, shape, 1)
        for slot in range(slots):
            rows = sum(one[slot] for one in grams) * (1.0 / snap_total)
            rows_r, rows_i = rows[: double // 2], rows[double // 2 :]
            rows_r = jnp.where(diagonal, rows_r + loading_level, rows_r)
            steer_r, steer_i = steer[slot, :half], steer[slot, half:]
            systems.append(joined_system(swept[slot, 0], swept[slot, 1], rows_r, rows_i, steer_r, steer_i, known))
        for slot, (real, imag) in enumerate(eliminate(systems, known, half, math.gcd(known, PIVOTS), AT_ONCE)):
            solved_r, solved_i = real[:, half:], imag[:, half:]
            power = jnp.sum(steer[slot, :half] * solved_r + steer[slot, half:] * solved_i, axis=0, keepdims=True)
            scale = 1.0 / jnp.sqrt(power)
            weight_r, weight_i = (solved_r * scale).T, (solved_i * scale).T
            mix[slot, :count] = jnp.concatenate([weight_r, weight_i], axis=1).astype(bf16)
            mix[slot, count:] = jnp.concatenate([-weight_i, weight_r], axis=1).astype(bf16)

    for slot in range(slots):

        @pl.when(pl.program_id(0) == slot)
        def _():
            mixed = jnp.dot(mix[slot], stacked_rows(blocks[slot], arrays), preferred_element_type=f32).astype(bf16)
            out[0, 0] = mixed[:count]
            out[0, 1] = mixed[count:]


def beams(snap_total, grams, swept, steer, blocks):
    slots, double, count = steer.shape
    arrays, numbered = flattened([block for one in blocks for block in one])
    per_slot = len(blocks[0])
    numbered = [numbered[i * per_slot : (i + 1) * per_slot] for i in range(slots)]
    snaps = sum(array.shape[-1] for array, _ in blocks[0][0])
    operands = [*grams, swept, steer, *arrays]
    return pl.pallas_call(
        functools.partial(beams_kernel, len(grams), snap_total, numbered),
        grid=(slots,),
        in_specs=[pl.BlockSpec(memory_space=pltpu.VMEM)] * len(operands),
        out_specs=pl.BlockSpec((1, 2, count, snaps), lambda i: (i, 0, 0, 0)),
        out_shape=jax.ShapeDtypeStruct((slots, 2, count, snaps), bf16),
        scratch_shapes=[pltpu.VMEM((slots, 2 * count, double), bf16)],
        compiler_params=pltpu.CompilerParams(vmem_limit_bytes=BEAMS_VMEM),
        cost_estimate=QUICK,
        name="beams",
    )(*operands)


def partners(value, axis, distance):
    length = lax.axis_size(axis)
    return lax.ppermute(value, axis, [(i, i ^ distance) for i in range(length)])


def segment_sums(packed):
    length = lax.axis_size("seg")
    if length <= 4:
        return [packed] + [partners(packed, "seg", d) for d in range(1, length)]
    distance = 1
    while distance < length:
        packed = packed + partners(packed, "seg", distance)
        distance *= 2
    return [packed]


def after(value, *earlier):
    return lax.optimization_barrier((value, *earlier))


def on_device(voltages, filter_taps, positions, beam_dirs, chan_table):
    stations, width, snaps = voltages.shape
    channels = chan_table.shape[0]
    owners = lax.axis_size("stn")
    segments = lax.axis_size("seg")
    slots = channels // owners
    half = owners * stations
    snap_total = snaps * segments
    near, far = list(range(1, owners // 2)), list(range(owners // 2, owners))
    order = list(range(owners))
    late_ones = far[len(far) // 2 :]
    known = (owners - len(late_ones)) * stations
    split = far[:1] + near[1:][: max(len(near) - 2, 1)]
    rest = [d for d in order if d not in split]
    layout = [[(slot, d) for slot in range(slots)] for d in split + rest]
    halo = lax.ppermute(voltages[:, :, snaps - LANES :], "seg", [(i, i + 1) for i in range(segments - 1)])
    second = channelize(slots, "second", order, layout, chan_table, voltages, filter_taps)
    late = [partners(one, "stn", d) for d, one in zip(split, second)]
    joined = {key: (one, i) for keys, one in zip(layout[len(split) :], second[len(split) :]) for i, key in enumerate(keys)}
    *first, steer = channelize(
        slots, "first", order, layout, chan_table, voltages, filter_taps, halo, positions, beam_dirs, joined
    )
    first, steer, late = after(first, steer, late)
    first = dict(zip(split + rest, first))
    arrived = {d: partners(first[d], "stn", d) for d in split + rest[1:] if d not in late_ones}
    following = {}
    for i, d in enumerate(late_ones):
        ahead = [far[i]] + [e for e in near if e in split][i :: len(late_ones)]
        value, there = after(first[d], [arrived[e] for e in ahead])
        arrived.update(zip(ahead, there))
        following[d] = partners(value, "stn", d)
    arrived.update({0: first[0], **following})
    held = {(slot, d): [(one, slot)] for d, one in arrived.items() for slot in range(slots)}
    for d, one in zip(split, late):
        for slot in range(slots):
            held[slot, d].append((one, slot))
    blocks = lambda ds: [[held[slot, d] for d in ds] for slot in range(slots)]
    grams = segment_sums(first_gram(blocks([d for d in order if d not in late_ones]), known, half))
    swept = first_solve(snap_total, grams, steer)
    following, swept = after(following, swept)
    held.update({(slot, d): [(one, slot)] for d, one in following.items() for slot in range(slots)})
    grams = segment_sums(last_gram(blocks(order), len(late_ones), half - known, half))
    return beams(snap_total, grams, swept, steer, blocks(order))


def solution(mesh):
    return jax.shard_map(
        on_device,
        mesh=mesh,
        in_specs=(P("stn", None, "seg"), P(), P(), P(), P()),
        out_specs=P("stn", None, None, "seg"),
        check_vma=False,
    )
```

```python
import functools
import math

import jax
import jax.numpy as jnp
from jax import lax
from jax.experimental import pallas as pl
from jax.experimental.pallas import tpu as pltpu
from jax.sharding import PartitionSpec as P

DIRS = 360
LANES = 128
GROUP = 8
PIVOTS = 16
QUICK = pl.CostEstimate(flops=1000, bytes_accessed=1000, transcendentals=0)
AT_ONCE = 4
VMEM_BYTES = 16 << 20
GRAM_VMEM = 8 << 20
BEAMS_VMEM = 12 << 20

loading_level = 0.1
full_turn = 2.0 * math.pi
NN = (((1,), (0,)), ((), ()))
NT = (((1,), (1,)), ((), ()))
TN = (((0,), (0,)), ((), ()))
f32, bf16 = jnp.float32, jnp.bfloat16


def split_in_two(value):
    high = value.astype(bf16)
    return high, (value - high.astype(f32)).astype(bf16)


def merged_rows(pieces):
    if all(piece.shape[0] % 16 == 0 for piece in pieces):
        return jnp.concatenate(pieces, axis=0)
    return jnp.concatenate([piece.astype(f32) for piece in pieces], axis=0).astype(bf16)


def dft_rows(channels, width):
    shape = (2 * len(channels), GROUP * width)
    row = lax.broadcasted_iota(jnp.int32, shape, 0)
    lane = lax.broadcasted_iota(jnp.int32, shape, 1)
    channel = jnp.zeros(shape, jnp.int32)
    for index, one in enumerate(channels):
        channel = jnp.where(row // 2 == index, one, channel)
    angle = lax.rem(channel * lax.rem(lane, width), width).astype(f32) * (full_turn / width)
    values = jnp.where(row % 2 == 0, jnp.cos(angle), -jnp.sin(angle))
    shape = (GROUP, GROUP * width)
    own = lax.broadcasted_iota(jnp.int32, shape, 1) // width == lax.broadcasted_iota(jnp.int32, shape, 0)
    spread = [jnp.where(own, jnp.broadcast_to(values[i : i + 1], shape), 0.0) for i in range(2 * len(channels))]
    return jnp.concatenate(spread, axis=0)


def steering(me, order, positions, beam_dirs, channel, channels):
    owners = len(order)
    stations = positions.shape[1] // owners
    columns = jnp.concatenate([positions, jnp.zeros((6, positions.shape[1]), f32)], axis=0).T
    span = 1
    while span < owners:
        parts = [columns[i * stations : (i + 1) * stations] for i in range(owners)]
        turned = jnp.concatenate([parts[i ^ span] for i in range(owners)], axis=0)
        columns = jnp.where((me & span) != 0, turned, columns)
        span *= 2
    columns = jnp.concatenate([columns[d * stations : (d + 1) * stations] for d in order], axis=0)
    bearing = beam_dirs.astype(f32) * (full_turn / DIRS)
    frequency = 1.0 + channel.astype(f32) / channels
    path_delay = columns[:, 0:1] * jnp.cos(bearing) + columns[:, 1:2] * jnp.sin(bearing)
    turns = frequency * path_delay
    phases = full_turn * (turns - jnp.round(turns))
    return jnp.concatenate([jnp.cos(phases), jnp.sin(phases)], axis=0)


def channelize_kernel(owners, slots, part, order, places, joined, other_count, *refs):
    count = owners * slots
    has_halo = part != "second"
    chans_in, volts, taps_in = refs[:3]
    others = refs[3 + 3 * has_halo : 3 + 3 * has_halo + other_count]
    outs = refs[3 + 3 * has_halo + other_count : len(refs) - 10]
    dft, held, high, low, chans, taps, sems, chans_sem, taps_sem, halo_sem = refs[-10:]
    stations, width, snaps = volts.shape
    chunk = held.shape[2] - LANES
    tap_count = taps.shape[0]
    step = tap_count // 2
    rows = 2 * GROUP
    half = count * rows
    pieces = sems.shape[0]
    piece = stations // pieces
    small = [pltpu.make_async_copy(chans_in, chans, chans_sem), pltpu.make_async_copy(taps_in, taps, taps_sem)]
    if has_halo:
        small.append(pltpu.make_async_copy(refs[3], held.at[:, :, :LANES], halo_sem))
    copies = []
    for index in range(pieces):
        members = pl.ds(index * piece, piece)
        if has_halo:
            source, target = volts.at[members, :, :chunk], held.at[members, :, LANES:]
        else:
            source, target = volts.at[members, :, snaps - chunk - LANES :], held.at[members]
        copies.append(pltpu.make_async_copy(source, target, sems.at[index]))
    for copy in small + copies:
        copy.start()
    for copy in small:
        copy.wait()

    me = lax.axis_index("stn")
    table = dft_rows([chans[(me ^ d) * slots + slot] for slot in range(slots) for d in range(owners)], width)
    dft[:half], dft[half:] = split_in_two(table)
    columns = taps[...].T
    tap = [jnp.broadcast_to(columns[:, m : m + 1], (width, chunk + LANES)) for m in range(tap_count)]
    results = []
    for station in range(stations):
        if station % piece == 0:
            copies[station // piece].wait()
        now = held[station]
        shifted = [(pltpu.roll(now, m, axis=1) if m else now).astype(f32) for m in range(step)]
        near = sum(tap[m] * shifted[m] for m in range(step))
        far = sum(tap[step + m] * shifted[m] for m in range(step))
        filtered = (near + pltpu.roll(far, step, axis=1))[:, LANES:]
        member = station % GROUP
        high[pl.ds(member * width, width), :], low[pl.ds(member * width, width), :] = split_in_two(filtered)
        if member == GROUP - 1:
            both = jnp.dot(dft[...], high[...], preferred_element_type=f32)
            cross = jnp.dot(dft[:half], low[...], preferred_element_type=f32)
            results.append(both[:half] + (both[half:] + cross))
    for index in range(count):
        slot, d = divmod(index, owners)
        number, entry = places[slot, d]
        target = outs[number].at[entry]
        for real in range(2):
            first = index * rows + real * GROUP
            merged = jnp.concatenate([one[first : first + GROUP] for one in results], axis=0)
            target[real, :, :chunk] = merged.astype(bf16)
        if (slot, d) in joined:
            at, inside = joined[slot, d]
            target[:, :, chunk:] = others[at][inside]
    if has_halo:
        for slot in range(slots):
            channel = chans[me * slots + slot]
            outs[-1][slot] = steering(me, order, refs[4][...], refs[5][...], channel, owners * slots)


def channelize(slots, part, order, layout, chans, volts, taps, halo=None, positions=None, beam_dirs=None, joined=None):
    stations, width, snaps = volts.shape
    owners = len(order)
    count = owners * slots
    chunk = snaps // 2
    pieces = max(stations // 4, 1)
    joined = joined or {}
    others = []
    for array, _ in joined.values():
        if not any(array is one for one in others):
            others.append(array)
    number_of = lambda array: next(i for i, one in enumerate(others) if one is array)
    joined = {key: (number_of(array), entry) for key, (array, entry) in joined.items()}
    places, out_shape = {}, []
    for number, keys in enumerate(layout):
        for entry, key in enumerate(keys):
            places[key] = (number, entry)
        length = snaps if keys[0] in joined else chunk
        out_shape.append(jax.ShapeDtypeStruct((len(keys), 2, stations, length), bf16))
    if halo is not None:
        out_shape.append(jax.ShapeDtypeStruct((slots, 2 * owners * stations, beam_dirs.shape[0]), f32))
    operands = [pltpu.with_memory_space_constraint(one, pltpu.HBM) for one in (chans, volts, taps)]
    operands += ([] if halo is None else [halo, positions, beam_dirs[None, :]]) + others
    return pl.pallas_call(
        functools.partial(channelize_kernel, owners, slots, part, order, places, joined, len(others)),
        in_specs=[pl.BlockSpec(memory_space=pltpu.HBM)] * 3
        + [pl.BlockSpec(memory_space=pl.ANY)] * (halo is not None)
        + [pl.BlockSpec(memory_space=pltpu.VMEM)] * (len(operands) - 3 - (halo is not None)),
        out_specs=[pl.BlockSpec(memory_space=pltpu.VMEM)] * len(out_shape),
        out_shape=out_shape,
        scratch_shapes=[
            pltpu.VMEM((4 * count * GROUP, GROUP * width), bf16),
            pltpu.VMEM((stations, width, chunk + LANES), bf16),
            pltpu.VMEM((GROUP * width, chunk), bf16),
            pltpu.VMEM((GROUP * width, chunk), bf16),
            pltpu.SMEM(chans.shape, jnp.int32),
            pltpu.VMEM(taps.shape, f32),
            pltpu.SemaphoreType.DMA((pieces,)),
            pltpu.SemaphoreType.DMA(()),
            pltpu.SemaphoreType.DMA(()),
            pltpu.SemaphoreType.DMA(()),
        ],
        compiler_params=pltpu.CompilerParams(vmem_limit_bytes=VMEM_BYTES),
        cost_estimate=QUICK,
        name="channelize_" + part,
    )(*operands)


def flattened(blocks):
    arrays, numbered = [], []
    for block in blocks:
        numbered.append([])
        for array, entry in block:
            found = [i for i, one in enumerate(arrays) if one is array]
            if not found:
                found = [len(arrays)]
                arrays.append(array)
            numbered[-1].append((found[0], entry))
    return arrays, numbered


def stacked_rows(blocks, refs):
    rows = []
    for part in range(2):
        for block in blocks:
            rows.append(jnp.concatenate([refs[at][entry, part] for at, entry in block], axis=1))
    return merged_rows(rows)


def first_gram_kernel(blocks, *refs):
    out = refs[-1]
    slots, half, wide = out.shape
    row = lax.broadcasted_iota(jnp.int32, (half, half), 0)
    column = lax.broadcasted_iota(jnp.int32, (half, half), 1)
    for slot in range(slots):
        stacked = stacked_rows(blocks[slot], refs[:-1])
        gram = lax.dot_general(stacked, stacked, NT, preferred_element_type=f32)
        sym_part = gram[:half, :half] + gram[half:, half:]
        skew_part = gram[half:, :half] - gram[:half, half:]
        packed = jnp.where(row >= column, sym_part, skew_part)
        out[slot] = jnp.concatenate([packed, jnp.zeros((half, wide - half), f32)], axis=1)


def last_gram_kernel(blocks, count, *refs):
    out = refs[-1]
    slots, double, half = out.shape
    rows = double // 2
    for slot in range(slots):
        stacked = stacked_rows(blocks[slot], refs[:-1])
        ours = stacked_rows(blocks[slot][-count:], refs[:-1])
        gram = lax.dot_general(ours, stacked, NT, preferred_element_type=f32)
        out[slot, :rows] = gram[:rows, :half] + gram[rows:, half:]
        out[slot, rows:] = gram[rows:, :half] - gram[:rows, half:]


def gram_call(kernel, blocks, shape, name):
    operands, numbered = flattened([block for one in blocks for block in one])
    per_slot = len(blocks[0])
    numbered = [numbered[i * per_slot : (i + 1) * per_slot] for i in range(len(blocks))]
    return pl.pallas_call(
        functools.partial(kernel, numbered),
        in_specs=[pl.BlockSpec(memory_space=pltpu.VMEM)] * len(operands),
        out_specs=pl.BlockSpec(memory_space=pltpu.VMEM),
        out_shape=jax.ShapeDtypeStruct((len(blocks), *shape), f32),
        compiler_params=pltpu.CompilerParams(vmem_limit_bytes=GRAM_VMEM),
        cost_estimate=QUICK,
        name=name,
    )(*operands)


def first_gram(blocks, stations, half):
    return gram_call(first_gram_kernel, blocks, (stations, half), "first_gram")


def last_gram(blocks, count, stations, half):
    kernel = lambda numbered, *refs: last_gram_kernel(numbered, count, *refs)
    return gram_call(kernel, blocks, (2 * stations, half), "last_gram")


def dot(left, right, dims=NN):
    return lax.dot_general(left, right, dims, precision=lax.Precision.HIGHEST, preferred_element_type=f32)


def split_in_three(value):
    high, rest = value.astype(bf16), value
    rest = rest - high.astype(f32)
    middle = rest.astype(bf16)
    return high, middle, (rest - middle.astype(f32)).astype(bf16)


def deep_dot(left, right):
    a, b = split_in_three(left), split_in_three(right)
    left = jnp.concatenate([a[0], a[0], a[1], a[1], a[0], a[2]], axis=0)
    right = jnp.concatenate([b[0], b[1], b[0], b[1], b[2], b[0]], axis=0)
    return lax.dot_general(left, right, TN, preferred_element_type=f32)


def sweep_rows(systems, lanes, at_once):
    count, width = systems[0][0].shape
    narrow = (count, LANES)
    index, index_wide = (lax.broadcasted_iota(jnp.int32, shape, 0) for shape in (narrow, (count, width)))
    repeated = lambda value: jnp.concatenate([value] * (width // LANES), axis=1)
    rows = list(systems)
    for start in range(0, count, at_once):
        fetched = lanes[start : start + at_once]
        columns = [
            [tuple(jnp.broadcast_to(part[:, lane : lane + 1], narrow) for part in row) for lane in fetched] for row in rows
        ]
        for j in range(len(fetched)):
            step = start + j
            spread = lambda value: jnp.broadcast_to(value[step : step + 1], value.shape)

            def swept(value, here, a, b, scale):
                real, imag = value
                pick_r, pick_i = spread(real) * scale, spread(imag) * scale
                return (
                    jnp.where(here, pick_r, real - (a * pick_r - b * pick_i)),
                    jnp.where(here, pick_i, imag - (a * pick_i + b * pick_r)),
                )

            scales = [1.0 / spread(column[j][0]) for column in columns]
            for later in range(j + 1, len(fetched)):
                for column, scale in zip(columns, scales):
                    column[later] = swept(column[later], index == step, *column[j], scale)
            for number, (column, scale) in enumerate(zip(columns, scales)):
                a, b = column[j]
                rows[number] = swept(rows[number], index_wide == step, repeated(a), repeated(b), repeated(scale))
    return rows


def eliminate(systems, start, stop, pivots, at_once):
    half = systems[0][0].shape[0]
    shape = systems[0][0].shape
    rank = lax.broadcasted_iota(jnp.int32, shape, 0)
    lane = lax.broadcasted_iota(jnp.int32, shape, 1)
    for first in range(start, stop, pivots):
        last = first + pivots
        tile = first // LANES * LANES
        inside = (lane[first:last] >= first) & (lane[first:last] < last)
        minus_one = jnp.where(rank[first:last] == lane[first:last], -1.0, 0.0)
        sides, rows = [], []
        for real, imag in systems:
            row_r, row_i = real[first:last], imag[first:last]
            upper = jnp.concatenate([row_r[:, :half], -row_i[:, :half]], axis=1)
            lower = jnp.concatenate([row_i[:, :half], row_r[:, :half]], axis=1)
            sides.append(jnp.concatenate([upper, lower], axis=0))
            rows.append((
                jnp.concatenate([row_r[:, tile : tile + LANES], jnp.where(inside, minus_one, row_r)], axis=1),
                jnp.concatenate([row_i[:, tile : tile + LANES], jnp.where(inside, 0.0, row_i)], axis=1),
            ))
        rows = sweep_rows(rows, range(first - tile, last - tile), at_once)
        own = (rank >= first) & (rank < last)
        gone = (lane >= first) & (lane < last)
        spread = lambda piece: jnp.concatenate([piece] * (half // pivots), axis=0)
        results = []
        for (real, imag), side, (row_r, row_i) in zip(systems, sides, rows):
            row_r, row_i = row_r[:, LANES:], row_i[:, LANES:]
            update = deep_dot(side, jnp.concatenate([row_r, row_i], axis=0))
            results.append((
                jnp.where(own, spread(row_r), jnp.where(gone, 0.0, real) - update[:half]),
                jnp.where(own, spread(row_i), jnp.where(gone, 0.0, imag) - update[half:]),
            ))
        systems = results
    return systems


def first_solve_kernel(segments, snap_total, *refs):
    grams, steer, out = refs[:segments], refs[segments], refs[-1]
    slots, stations, half = grams[0].shape
    row = lax.broadcasted_iota(jnp.int32, (half, half), 0)
    column = lax.broadcasted_iota(jnp.int32, (half, half), 1)
    systems = []
    for slot in range(slots):
        packed = sum(one[slot] for one in grams) * (1.0 / snap_total)
        if stations < half:
            packed = jnp.concatenate([packed, jnp.zeros((half - stations, half), f32)], axis=0)
        turned = packed.T
        real = jnp.where(row >= column, packed, turned)
        real = jnp.where((row == column) & (row < stations), real + loading_level, real)
        imag = jnp.where(row < column, packed, jnp.where(row > column, -turned, 0.0))
        known = row < stations
        systems.append((
            jnp.concatenate([real, jnp.where(known, steer[slot, :half], 0.0)], axis=1),
            jnp.concatenate([imag, jnp.where(known, steer[slot, half:], 0.0)], axis=1),
        ))
    for slot, (real, imag) in enumerate(eliminate(systems, 0, stations, math.gcd(stations, PIVOTS), AT_ONCE)):
        out[slot, 0] = jnp.concatenate([real, systems[slot][0][:, :half]], axis=1)
        out[slot, 1] = jnp.concatenate([imag, systems[slot][1][:, :half]], axis=1)


def first_solve(snap_total, grams, steer):
    slots, _, count = steer.shape
    half = grams[0].shape[2]
    return pl.pallas_call(
        functools.partial(first_solve_kernel, len(grams), snap_total),
        in_specs=[pl.BlockSpec(memory_space=pltpu.VMEM)] * (len(grams) + 1),
        out_specs=pl.BlockSpec(memory_space=pltpu.VMEM),
        out_shape=jax.ShapeDtypeStruct((slots, 2, half, 2 * half + count), f32),
        compiler_params=pltpu.CompilerParams(vmem_limit_bytes=BEAMS_VMEM),
        cost_estimate=QUICK,
        name="first_solve",
    )(*grams, steer)


def complex_rows(real, imag):
    upper = jnp.concatenate([real, -imag], axis=1)
    return jnp.concatenate([upper, jnp.concatenate([imag, real], axis=1)], axis=0)


def joined_system(swept_r, swept_i, rows_r, rows_i, steer_r, steer_i, known):
    count, half = rows_r.shape
    end = half + steer_r.shape[1]
    lane = lax.broadcasted_iota(jnp.int32, rows_r.shape, 1)
    cross_r, cross_i = jnp.where(lane < known, rows_r, 0.0), jnp.where(lane < known, rows_i, 0.0)
    stacked = lambda first, last: jnp.concatenate([swept_r[:, first:last], swept_i[:, first:last]], axis=0)
    inverse, matrix = stacked(0, half), stacked(end, end + half)
    guess = -dot(complex_rows(cross_r, cross_i), inverse)
    rest = jnp.concatenate([cross_r, cross_i], axis=0) - dot(complex_rows(guess[:count], guess[count:]), matrix)
    guess = guess - dot(complex_rows(rest[:count], rest[count:]), inverse)
    turn_r, turn_i = guess[:count], guess[count:]
    ahead = lax.broadcasted_iota(jnp.int32, steer_r.shape, 0) < known
    first_steer = jnp.concatenate([jnp.where(ahead, steer_r, 0.0), jnp.where(ahead, steer_i, 0.0)], axis=0)
    taken = dot(complex_rows(turn_r, turn_i), first_steer)
    back_r, back_i = steer_r[known:] - taken[:count], steer_i[known:] - taken[count:]
    left = jnp.concatenate(
        [jnp.concatenate([turn_r, turn_i], axis=1), jnp.concatenate([turn_i, -turn_r], axis=1)], axis=0
    )
    right = jnp.concatenate([jnp.zeros((known, 2 * half), f32), jnp.concatenate([cross_r, cross_i], axis=1)], axis=0)
    inner = dot(left, right, NT)
    rows_r = jnp.where(lane < known, turn_r, rows_r - inner[:count])
    rows_i = jnp.where(lane < known, turn_i, rows_i - inner[count:])
    real = jnp.concatenate([swept_r[:known, :end], jnp.concatenate([rows_r, back_r], axis=1)], axis=0)
    imag = jnp.concatenate([swept_i[:known, :end], jnp.concatenate([rows_i, back_i], axis=1)], axis=0)
    return real, imag


def beams_kernel(segments, snap_total, blocks, *refs):
    grams, swept, steer = refs[:segments], refs[segments], refs[segments + 1]
    arrays, out, mix = refs[segments + 2 : -2], refs[-2], refs[-1]
    slots, double, half = grams[0].shape
    known = half - double // 2
    count = steer.shape[2]

    @pl.when(pl.program_id(0) == 0)
    def _():
        systems = []
        shape = (double // 2, half)
        diagonal = lax.broadcasted_iota(jnp.int32, shape, 0) + known == lax.broadcasted_iota(jnp.int32, shape, 1)
        for slot in range(slots):
            rows = sum(one[slot] for one in grams) * (1.0 / snap_total)
            rows_r, rows_i = rows[: double // 2], rows[double // 2 :]
            rows_r = jnp.where(diagonal, rows_r + loading_level, rows_r)
            steer_r, steer_i = steer[slot, :half], steer[slot, half:]
            systems.append(joined_system(swept[slot, 0], swept[slot, 1], rows_r, rows_i, steer_r, steer_i, known))
        for slot, (real, imag) in enumerate(eliminate(systems, known, half, math.gcd(known, PIVOTS), AT_ONCE)):
            solved_r, solved_i = real[:, half:], imag[:, half:]
            power = jnp.sum(steer[slot, :half] * solved_r + steer[slot, half:] * solved_i, axis=0, keepdims=True)
            scale = 1.0 / jnp.sqrt(power)
            weight_r, weight_i = (solved_r * scale).T, (solved_i * scale).T
            mix[slot, :count] = jnp.concatenate([weight_r, weight_i], axis=1).astype(bf16)
            mix[slot, count:] = jnp.concatenate([-weight_i, weight_r], axis=1).astype(bf16)

    for slot in range(slots):

        @pl.when(pl.program_id(0) == slot)
        def _():
            mixed = jnp.dot(mix[slot], stacked_rows(blocks[slot], arrays), preferred_element_type=f32).astype(bf16)
            out[0, 0] = mixed[:count]
            out[0, 1] = mixed[count:]


def beams(snap_total, grams, swept, steer, blocks):
    slots, double, count = steer.shape
    arrays, numbered = flattened([block for one in blocks for block in one])
    per_slot = len(blocks[0])
    numbered = [numbered[i * per_slot : (i + 1) * per_slot] for i in range(slots)]
    snaps = sum(array.shape[-1] for array, _ in blocks[0][0])
    operands = [*grams, swept, steer, *arrays]
    return pl.pallas_call(
        functools.partial(beams_kernel, len(grams), snap_total, numbered),
        grid=(slots,),
        in_specs=[pl.BlockSpec(memory_space=pltpu.VMEM)] * len(operands),
        out_specs=pl.BlockSpec((1, 2, count, snaps), lambda i: (i, 0, 0, 0)),
        out_shape=jax.ShapeDtypeStruct((slots, 2, count, snaps), bf16),
        scratch_shapes=[pltpu.VMEM((slots, 2 * count, double), bf16)],
        compiler_params=pltpu.CompilerParams(vmem_limit_bytes=BEAMS_VMEM),
        cost_estimate=QUICK,
        name="beams",
    )(*operands)


def partners(value, axis, distance):
    length = lax.axis_size(axis)
    return lax.ppermute(value, axis, [(i, i ^ distance) for i in range(length)])


def segment_sums(packed):
    length = lax.axis_size("seg")
    if length <= 4:
        return [packed] + [partners(packed, "seg", d) for d in range(1, length)]
    distance = 1
    while distance < length:
        packed = packed + partners(packed, "seg", distance)
        distance *= 2
    return [packed]


def after(value, *earlier):
    return lax.optimization_barrier((value, *earlier))


def on_device(voltages, filter_taps, positions, beam_dirs, chan_table):
    stations, width, snaps = voltages.shape
    channels = chan_table.shape[0]
    owners = lax.axis_size("stn")
    segments = lax.axis_size("seg")
    slots = channels // owners
    half = owners * stations
    snap_total = snaps * segments
    near, far = list(range(1, owners // 2)), list(range(owners // 2, owners))
    order = list(range(owners))
    late_ones = far[len(far) // 2 :]
    known = (owners - len(late_ones)) * stations
    split = far[:1] + near[1:] + far[1:2]
    rest = [d for d in order if d not in split]
    layout = [[(slot, d) for slot in range(slots)] for d in split + rest]
    halo = lax.ppermute(voltages[:, :, snaps - LANES :], "seg", [(i, i + 1) for i in range(segments - 1)])
    second = channelize(slots, "second", order, layout, chan_table, voltages, filter_taps)
    late = [partners(one, "stn", d) for d, one in zip(split, second)]
    joined = {key: (one, i) for keys, one in zip(layout[len(split) :], second[len(split) :]) for i, key in enumerate(keys)}
    *first, steer = channelize(
        slots, "first", order, layout, chan_table, voltages, filter_taps, halo, positions, beam_dirs, joined
    )
    at = len(split) - 1
    first, steer, late[:at] = after(first, steer, late[:at])
    first[at], late[at] = after(first[at], late[at])
    first = dict(zip(split + rest, first))
    arrived = {d: partners(first[d], "stn", d) for d in split + rest[1:] if d not in late_ones}
    following = {}
    for i, d in enumerate(late_ones):
        ahead = [far[i]] + (near[1:] if d == far[-1] else [])
        value, there = after(first[d], [arrived[e] for e in ahead])
        arrived.update(zip(ahead, there))
        following[d] = partners(value, "stn", d)
    arrived.update({0: first[0], **following})
    held = {(slot, d): [(one, slot)] for d, one in arrived.items() for slot in range(slots)}
    for d, one in zip(split, late):
        for slot in range(slots):
            held[slot, d].append((one, slot))
    blocks = lambda ds: [[held[slot, d] for d in ds] for slot in range(slots)]
    grams = segment_sums(first_gram(blocks([d for d in order if d not in late_ones]), known, half))
    swept = first_solve(snap_total, grams, steer)
    following, swept = after(following, swept)
    held.update({(slot, d): [(one, slot)] for d, one in following.items() for slot in range(slots)})
    grams = segment_sums(last_gram(blocks(order), len(late_ones), half - known, half))
    return beams(snap_total, grams, swept, steer, blocks(order))


def solution(mesh):
    return jax.shard_map(
        on_device,
        mesh=mesh,
        in_specs=(P("stn", None, "seg"), P(), P(), P(), P()),
        out_specs=P("stn", None, None, "seg"),
        check_vma=False,
    )
```

```python
import functools
import math

import jax
import jax.numpy as jnp
from jax import lax
from jax.experimental import pallas as pl
from jax.experimental.pallas import tpu as pltpu
from jax.sharding import PartitionSpec as P

DIRS = 360
LANES = 128
GROUP = 8
PIVOTS = 16
QUICK = pl.CostEstimate(flops=1000, bytes_accessed=1000, transcendentals=0)
AT_ONCE = 4
VMEM_BYTES = 16 << 20
GRAM_VMEM = 8 << 20
BEAMS_VMEM = 12 << 20

loading_level = 0.1
full_turn = 2.0 * math.pi
NN = (((1,), (0,)), ((), ()))
NT = (((1,), (1,)), ((), ()))
TN = (((0,), (0,)), ((), ()))
f32, bf16 = jnp.float32, jnp.bfloat16


def split_in_two(value):
    high = value.astype(bf16)
    return high, (value - high.astype(f32)).astype(bf16)


def merged_rows(pieces):
    if all(piece.shape[0] % 16 == 0 for piece in pieces):
        return jnp.concatenate(pieces, axis=0)
    return jnp.concatenate([piece.astype(f32) for piece in pieces], axis=0).astype(bf16)


def dft_rows(channels, width):
    shape = (2 * len(channels), GROUP * width)
    row = lax.broadcasted_iota(jnp.int32, shape, 0)
    lane = lax.broadcasted_iota(jnp.int32, shape, 1)
    channel = jnp.zeros(shape, jnp.int32)
    for index, one in enumerate(channels):
        channel = jnp.where(row // 2 == index, one, channel)
    angle = lax.rem(channel * lax.rem(lane, width), width).astype(f32) * (full_turn / width)
    values = jnp.where(row % 2 == 0, jnp.cos(angle), -jnp.sin(angle))
    shape = (GROUP, GROUP * width)
    own = lax.broadcasted_iota(jnp.int32, shape, 1) // width == lax.broadcasted_iota(jnp.int32, shape, 0)
    spread = [jnp.where(own, jnp.broadcast_to(values[i : i + 1], shape), 0.0) for i in range(2 * len(channels))]
    return jnp.concatenate(spread, axis=0)


def steering(me, order, positions, beam_dirs, channel, channels):
    owners = len(order)
    stations = positions.shape[1] // owners
    columns = jnp.concatenate([positions, jnp.zeros((6, positions.shape[1]), f32)], axis=0).T
    span = 1
    while span < owners:
        parts = [columns[i * stations : (i + 1) * stations] for i in range(owners)]
        turned = jnp.concatenate([parts[i ^ span] for i in range(owners)], axis=0)
        columns = jnp.where((me & span) != 0, turned, columns)
        span *= 2
    columns = jnp.concatenate([columns[d * stations : (d + 1) * stations] for d in order], axis=0)
    bearing = beam_dirs.astype(f32) * (full_turn / DIRS)
    frequency = 1.0 + channel.astype(f32) / channels
    path_delay = columns[:, 0:1] * jnp.cos(bearing) + columns[:, 1:2] * jnp.sin(bearing)
    turns = frequency * path_delay
    phases = full_turn * (turns - jnp.round(turns))
    return jnp.concatenate([jnp.cos(phases), jnp.sin(phases)], axis=0)


def channelize_kernel(owners, slots, part, order, places, joined, other_count, *refs):
    count = owners * slots
    has_halo = part != "second"
    chans_in, volts, taps_in = refs[:3]
    others = refs[3 + 3 * has_halo : 3 + 3 * has_halo + other_count]
    outs = refs[3 + 3 * has_halo + other_count : len(refs) - 10]
    dft, held, high, low, chans, taps, sems, chans_sem, taps_sem, halo_sem = refs[-10:]
    stations, width, snaps = volts.shape
    chunk = held.shape[2] - LANES
    tap_count = taps.shape[0]
    step = tap_count // 2
    rows = 2 * GROUP
    half = count * rows
    pieces = sems.shape[0]
    piece = stations // pieces
    small = [pltpu.make_async_copy(chans_in, chans, chans_sem), pltpu.make_async_copy(taps_in, taps, taps_sem)]
    if has_halo:
        small.append(pltpu.make_async_copy(refs[3], held.at[:, :, :LANES], halo_sem))
    copies = []
    for index in range(pieces):
        members = pl.ds(index * piece, piece)
        if has_halo:
            source, target = volts.at[members, :, :chunk], held.at[members, :, LANES:]
        else:
            source, target = volts.at[members, :, snaps - chunk - LANES :], held.at[members]
        copies.append(pltpu.make_async_copy(source, target, sems.at[index]))
    for copy in small + copies:
        copy.start()
    for copy in small:
        copy.wait()

    me = lax.axis_index("stn")
    table = dft_rows([chans[(me ^ d) * slots + slot] for slot in range(slots) for d in range(owners)], width)
    dft[:half], dft[half:] = split_in_two(table)
    columns = taps[...].T
    tap = [jnp.broadcast_to(columns[:, m : m + 1], (width, chunk + LANES)) for m in range(tap_count)]
    results = []
    for station in range(stations):
        if station % piece == 0:
            copies[station // piece].wait()
        now = held[station]
        shifted = [(pltpu.roll(now, m, axis=1) if m else now).astype(f32) for m in range(step)]
        near = sum(tap[m] * shifted[m] for m in range(step))
        far = sum(tap[step + m] * shifted[m] for m in range(step))
        filtered = (near + pltpu.roll(far, step, axis=1))[:, LANES:]
        member = station % GROUP
        high[pl.ds(member * width, width), :], low[pl.ds(member * width, width), :] = split_in_two(filtered)
        if member == GROUP - 1:
            both = jnp.dot(dft[...], high[...], preferred_element_type=f32)
            cross = jnp.dot(dft[:half], low[...], preferred_element_type=f32)
            results.append(both[:half] + (both[half:] + cross))
    for index in range(count):
        slot, d = divmod(index, owners)
        number, entry = places[slot, d]
        target = outs[number].at[entry]
        for real in range(2):
            first = index * rows + real * GROUP
            merged = jnp.concatenate([one[first : first + GROUP] for one in results], axis=0)
            target[real, :, :chunk] = merged.astype(bf16)
        if (slot, d) in joined:
            at, inside = joined[slot, d]
            target[:, :, chunk:] = others[at][inside]
    if has_halo:
        for slot in range(slots):
            channel = chans[me * slots + slot]
            outs[-1][slot] = steering(me, order, refs[4][...], refs[5][...], channel, owners * slots)


def channelize(slots, part, order, layout, chans, volts, taps, halo=None, positions=None, beam_dirs=None, joined=None):
    stations, width, snaps = volts.shape
    owners = len(order)
    count = owners * slots
    chunk = snaps // 2
    pieces = max(stations // 4, 1)
    joined = joined or {}
    others = []
    for array, _ in joined.values():
        if not any(array is one for one in others):
            others.append(array)
    number_of = lambda array: next(i for i, one in enumerate(others) if one is array)
    joined = {key: (number_of(array), entry) for key, (array, entry) in joined.items()}
    places, out_shape = {}, []
    for number, keys in enumerate(layout):
        for entry, key in enumerate(keys):
            places[key] = (number, entry)
        length = snaps if keys[0] in joined else chunk
        out_shape.append(jax.ShapeDtypeStruct((len(keys), 2, stations, length), bf16))
    if halo is not None:
        out_shape.append(jax.ShapeDtypeStruct((slots, 2 * owners * stations, beam_dirs.shape[0]), f32))
    operands = [pltpu.with_memory_space_constraint(one, pltpu.HBM) for one in (chans, volts, taps)]
    operands += ([] if halo is None else [halo, positions, beam_dirs[None, :]]) + others
    return pl.pallas_call(
        functools.partial(channelize_kernel, owners, slots, part, order, places, joined, len(others)),
        in_specs=[pl.BlockSpec(memory_space=pltpu.HBM)] * 3
        + [pl.BlockSpec(memory_space=pl.ANY)] * (halo is not None)
        + [pl.BlockSpec(memory_space=pltpu.VMEM)] * (len(operands) - 3 - (halo is not None)),
        out_specs=[pl.BlockSpec(memory_space=pltpu.VMEM)] * len(out_shape),
        out_shape=out_shape,
        scratch_shapes=[
            pltpu.VMEM((4 * count * GROUP, GROUP * width), bf16),
            pltpu.VMEM((stations, width, chunk + LANES), bf16),
            pltpu.VMEM((GROUP * width, chunk), bf16),
            pltpu.VMEM((GROUP * width, chunk), bf16),
            pltpu.SMEM(chans.shape, jnp.int32),
            pltpu.VMEM(taps.shape, f32),
            pltpu.SemaphoreType.DMA((pieces,)),
            pltpu.SemaphoreType.DMA(()),
            pltpu.SemaphoreType.DMA(()),
            pltpu.SemaphoreType.DMA(()),
        ],
        compiler_params=pltpu.CompilerParams(vmem_limit_bytes=VMEM_BYTES),
        cost_estimate=QUICK,
        name="channelize_" + part,
    )(*operands)


def flattened(blocks):
    arrays, numbered = [], []
    for block in blocks:
        numbered.append([])
        for array, entry in block:
            found = [i for i, one in enumerate(arrays) if one is array]
            if not found:
                found = [len(arrays)]
                arrays.append(array)
            numbered[-1].append((found[0], entry))
    return arrays, numbered


def stacked_rows(blocks, refs):
    rows = []
    for part in range(2):
        for block in blocks:
            rows.append(jnp.concatenate([refs[at][entry, part] for at, entry in block], axis=1))
    return merged_rows(rows)


def first_gram_kernel(blocks, *refs):
    out = refs[-1]
    slots, half, wide = out.shape
    row = lax.broadcasted_iota(jnp.int32, (half, half), 0)
    column = lax.broadcasted_iota(jnp.int32, (half, half), 1)
    for slot in range(slots):
        stacked = stacked_rows(blocks[slot], refs[:-1])
        gram = lax.dot_general(stacked, stacked, NT, preferred_element_type=f32)
        sym_part = gram[:half, :half] + gram[half:, half:]
        skew_part = gram[half:, :half] - gram[:half, half:]
        packed = jnp.where(row >= column, sym_part, skew_part)
        out[slot] = jnp.concatenate([packed, jnp.zeros((half, wide - half), f32)], axis=1)


def last_gram_kernel(blocks, count, *refs):
    out = refs[-1]
    slots, double, half = out.shape
    rows = double // 2
    for slot in range(slots):
        stacked = stacked_rows(blocks[slot], refs[:-1])
        ours = stacked_rows(blocks[slot][-count:], refs[:-1])
        gram = lax.dot_general(ours, stacked, NT, preferred_element_type=f32)
        out[slot, :rows] = gram[:rows, :half] + gram[rows:, half:]
        out[slot, rows:] = gram[rows:, :half] - gram[:rows, half:]


def gram_call(kernel, blocks, shape, name):
    operands, numbered = flattened([block for one in blocks for block in one])
    per_slot = len(blocks[0])
    numbered = [numbered[i * per_slot : (i + 1) * per_slot] for i in range(len(blocks))]
    return pl.pallas_call(
        functools.partial(kernel, numbered),
        in_specs=[pl.BlockSpec(memory_space=pltpu.VMEM)] * len(operands),
        out_specs=pl.BlockSpec(memory_space=pltpu.VMEM),
        out_shape=jax.ShapeDtypeStruct((len(blocks), *shape), f32),
        compiler_params=pltpu.CompilerParams(vmem_limit_bytes=GRAM_VMEM),
        cost_estimate=QUICK,
        name=name,
    )(*operands)


def first_gram(blocks, stations, half):
    return gram_call(first_gram_kernel, blocks, (stations, half), "first_gram")


def last_gram(blocks, count, stations, half):
    kernel = lambda numbered, *refs: last_gram_kernel(numbered, count, *refs)
    return gram_call(kernel, blocks, (2 * stations, half), "last_gram")


def dot(left, right, dims=NN):
    return lax.dot_general(left, right, dims, precision=lax.Precision.HIGHEST, preferred_element_type=f32)


def split_in_three(value):
    high, rest = value.astype(bf16), value
    rest = rest - high.astype(f32)
    middle = rest.astype(bf16)
    return high, middle, (rest - middle.astype(f32)).astype(bf16)


def deep_dot(left, right):
    a, b = split_in_three(left), split_in_three(right)
    left = jnp.concatenate([a[0], a[0], a[1], a[1], a[0], a[2]], axis=0)
    right = jnp.concatenate([b[0], b[1], b[0], b[1], b[2], b[0]], axis=0)
    return lax.dot_general(left, right, TN, preferred_element_type=f32)


def sweep_rows(systems, lanes, at_once):
    count, width = systems[0][0].shape
    narrow = (count, LANES)
    index, index_wide = (lax.broadcasted_iota(jnp.int32, shape, 0) for shape in (narrow, (count, width)))
    repeated = lambda value: jnp.concatenate([value] * (width // LANES), axis=1)
    rows = list(systems)
    for start in range(0, count, at_once):
        fetched = lanes[start : start + at_once]
        columns = [
            [tuple(jnp.broadcast_to(part[:, lane : lane + 1], narrow) for part in row) for lane in fetched] for row in rows
        ]
        for j in range(len(fetched)):
            step = start + j
            spread = lambda value: jnp.broadcast_to(value[step : step + 1], value.shape)

            def swept(value, here, a, b, scale):
                real, imag = value
                pick_r, pick_i = spread(real) * scale, spread(imag) * scale
                return (
                    jnp.where(here, pick_r, real - (a * pick_r - b * pick_i)),
                    jnp.where(here, pick_i, imag - (a * pick_i + b * pick_r)),
                )

            scales = [1.0 / spread(column[j][0]) for column in columns]
            for later in range(j + 1, len(fetched)):
                for column, scale in zip(columns, scales):
                    column[later] = swept(column[later], index == step, *column[j], scale)
            for number, (column, scale) in enumerate(zip(columns, scales)):
                a, b = column[j]
                rows[number] = swept(rows[number], index_wide == step, repeated(a), repeated(b), repeated(scale))
    return rows


def eliminate(systems, start, stop, pivots, at_once):
    half = systems[0][0].shape[0]
    shape = systems[0][0].shape
    rank = lax.broadcasted_iota(jnp.int32, shape, 0)
    lane = lax.broadcasted_iota(jnp.int32, shape, 1)
    for first in range(start, stop, pivots):
        last = first + pivots
        tile = first // LANES * LANES
        inside = (lane[first:last] >= first) & (lane[first:last] < last)
        minus_one = jnp.where(rank[first:last] == lane[first:last], -1.0, 0.0)
        sides, rows = [], []
        for real, imag in systems:
            row_r, row_i = real[first:last], imag[first:last]
            upper = jnp.concatenate([row_r[:, :half], -row_i[:, :half]], axis=1)
            lower = jnp.concatenate([row_i[:, :half], row_r[:, :half]], axis=1)
            sides.append(jnp.concatenate([upper, lower], axis=0))
            rows.append((
                jnp.concatenate([row_r[:, tile : tile + LANES], jnp.where(inside, minus_one, row_r)], axis=1),
                jnp.concatenate([row_i[:, tile : tile + LANES], jnp.where(inside, 0.0, row_i)], axis=1),
            ))
        rows = sweep_rows(rows, range(first - tile, last - tile), at_once)
        own = (rank >= first) & (rank < last)
        gone = (lane >= first) & (lane < last)
        spread = lambda piece: jnp.concatenate([piece] * (half // pivots), axis=0)
        results = []
        for (real, imag), side, (row_r, row_i) in zip(systems, sides, rows):
            row_r, row_i = row_r[:, LANES:], row_i[:, LANES:]
            update = deep_dot(side, jnp.concatenate([row_r, row_i], axis=0))
            results.append((
                jnp.where(own, spread(row_r), jnp.where(gone, 0.0, real) - update[:half]),
                jnp.where(own, spread(row_i), jnp.where(gone, 0.0, imag) - update[half:]),
            ))
        systems = results
    return systems


def first_solve_kernel(segments, snap_total, *refs):
    grams, steer, out = refs[:segments], refs[segments], refs[-1]
    slots, stations, half = grams[0].shape
    row = lax.broadcasted_iota(jnp.int32, (half, half), 0)
    column = lax.broadcasted_iota(jnp.int32, (half, half), 1)
    systems = []
    for slot in range(slots):
        packed = sum(one[slot] for one in grams) * (1.0 / snap_total)
        if stations < half:
            packed = jnp.concatenate([packed, jnp.zeros((half - stations, half), f32)], axis=0)
        turned = packed.T
        real = jnp.where(row >= column, packed, turned)
        real = jnp.where((row == column) & (row < stations), real + loading_level, real)
        imag = jnp.where(row < column, packed, jnp.where(row > column, -turned, 0.0))
        known = row < stations
        systems.append((
            jnp.concatenate([real, jnp.where(known, steer[slot, :half], 0.0)], axis=1),
            jnp.concatenate([imag, jnp.where(known, steer[slot, half:], 0.0)], axis=1),
        ))
    for slot, (real, imag) in enumerate(eliminate(systems, 0, stations, math.gcd(stations, PIVOTS), AT_ONCE)):
        out[slot, 0] = jnp.concatenate([real, systems[slot][0][:, :half]], axis=1)
        out[slot, 1] = jnp.concatenate([imag, systems[slot][1][:, :half]], axis=1)


def first_solve(snap_total, grams, steer):
    slots, _, count = steer.shape
    half = grams[0].shape[2]
    return pl.pallas_call(
        functools.partial(first_solve_kernel, len(grams), snap_total),
        in_specs=[pl.BlockSpec(memory_space=pltpu.VMEM)] * (len(grams) + 1),
        out_specs=pl.BlockSpec(memory_space=pltpu.VMEM),
        out_shape=jax.ShapeDtypeStruct((slots, 2, half, 2 * half + count), f32),
        compiler_params=pltpu.CompilerParams(vmem_limit_bytes=BEAMS_VMEM),
        cost_estimate=QUICK,
        name="first_solve",
    )(*grams, steer)


def complex_rows(real, imag):
    upper = jnp.concatenate([real, -imag], axis=1)
    return jnp.concatenate([upper, jnp.concatenate([imag, real], axis=1)], axis=0)


def joined_system(swept_r, swept_i, rows_r, rows_i, steer_r, steer_i, known):
    count, half = rows_r.shape
    end = half + steer_r.shape[1]
    lane = lax.broadcasted_iota(jnp.int32, rows_r.shape, 1)
    cross_r, cross_i = jnp.where(lane < known, rows_r, 0.0), jnp.where(lane < known, rows_i, 0.0)
    stacked = lambda first, last: jnp.concatenate([swept_r[:, first:last], swept_i[:, first:last]], axis=0)
    inverse, matrix = stacked(0, half), stacked(end, end + half)
    guess = -dot(complex_rows(cross_r, cross_i), inverse)
    rest = jnp.concatenate([cross_r, cross_i], axis=0) - dot(complex_rows(guess[:count], guess[count:]), matrix)
    guess = guess - dot(complex_rows(rest[:count], rest[count:]), inverse)
    turn_r, turn_i = guess[:count], guess[count:]
    ahead = lax.broadcasted_iota(jnp.int32, steer_r.shape, 0) < known
    first_steer = jnp.concatenate([jnp.where(ahead, steer_r, 0.0), jnp.where(ahead, steer_i, 0.0)], axis=0)
    taken = dot(complex_rows(turn_r, turn_i), first_steer)
    back_r, back_i = steer_r[known:] - taken[:count], steer_i[known:] - taken[count:]
    left = jnp.concatenate(
        [jnp.concatenate([turn_r, turn_i], axis=1), jnp.concatenate([turn_i, -turn_r], axis=1)], axis=0
    )
    right = jnp.concatenate([jnp.zeros((known, 2 * half), f32), jnp.concatenate([cross_r, cross_i], axis=1)], axis=0)
    inner = dot(left, right, NT)
    rows_r = jnp.where(lane < known, turn_r, rows_r - inner[:count])
    rows_i = jnp.where(lane < known, turn_i, rows_i - inner[count:])
    real = jnp.concatenate([swept_r[:known, :end], jnp.concatenate([rows_r, back_r], axis=1)], axis=0)
    imag = jnp.concatenate([swept_i[:known, :end], jnp.concatenate([rows_i, back_i], axis=1)], axis=0)
    return real, imag


def beams_kernel(segments, snap_total, blocks, *refs):
    grams, swept, steer = refs[:segments], refs[segments], refs[segments + 1]
    arrays, (out, mix, mixed_beams, sems) = refs[segments + 2 : -4], refs[-4:]
    slots, double, half = grams[0].shape
    known = half - double // 2
    count = steer.shape[2]

    systems = []
    shape = (double // 2, half)
    diagonal = lax.broadcasted_iota(jnp.int32, shape, 0) + known == lax.broadcasted_iota(jnp.int32, shape, 1)
    for slot in range(slots):
        rows = sum(one[slot] for one in grams) * (1.0 / snap_total)
        rows_r, rows_i = rows[: double // 2], rows[double // 2 :]
        rows_r = jnp.where(diagonal, rows_r + loading_level, rows_r)
        steer_r, steer_i = steer[slot, :half], steer[slot, half:]
        systems.append(joined_system(swept[slot, 0], swept[slot, 1], rows_r, rows_i, steer_r, steer_i, known))
    for slot, (real, imag) in enumerate(eliminate(systems, known, half, math.gcd(known, PIVOTS), AT_ONCE)):
        solved_r, solved_i = real[:, half:], imag[:, half:]
        power = jnp.sum(steer[slot, :half] * solved_r + steer[slot, half:] * solved_i, axis=0, keepdims=True)
        scale = 1.0 / jnp.sqrt(power)
        weight_r, weight_i = (solved_r * scale).T, (solved_i * scale).T
        mix[slot, :count] = jnp.concatenate([weight_r, weight_i], axis=1).astype(bf16)
        mix[slot, count:] = jnp.concatenate([-weight_i, weight_r], axis=1).astype(bf16)

    copies = []
    for slot in range(slots):
        stacked = stacked_rows(blocks[slot], arrays)
        for part in range(2):
            rows = mix[slot, part * count : (part + 1) * count]
            mixed_beams[slot, part] = jnp.dot(rows, stacked, preferred_element_type=f32).astype(bf16)
            copies.append(pltpu.make_async_copy(mixed_beams.at[slot, part], out.at[slot, part], sems.at[slot, part]))
            copies[-1].start()
    for copy in copies:
        copy.wait()


def beams(snap_total, grams, swept, steer, blocks):
    slots, double, count = steer.shape
    arrays, numbered = flattened([block for one in blocks for block in one])
    per_slot = len(blocks[0])
    numbered = [numbered[i * per_slot : (i + 1) * per_slot] for i in range(slots)]
    snaps = sum(array.shape[-1] for array, _ in blocks[0][0])
    operands = [*grams, swept, steer, *arrays]
    return pl.pallas_call(
        functools.partial(beams_kernel, len(grams), snap_total, numbered),
        in_specs=[pl.BlockSpec(memory_space=pltpu.VMEM)] * len(operands),
        out_specs=pl.BlockSpec(memory_space=pltpu.HBM),
        out_shape=jax.ShapeDtypeStruct((slots, 2, count, snaps), bf16),
        scratch_shapes=[
            pltpu.VMEM((slots, 2 * count, double), bf16),
            pltpu.VMEM((slots, 2, count, snaps), bf16),
            pltpu.SemaphoreType.DMA((slots, 2)),
        ],
        compiler_params=pltpu.CompilerParams(vmem_limit_bytes=BEAMS_VMEM),
        cost_estimate=QUICK,
        name="beams",
    )(*operands)


def partners(value, axis, distance):
    length = lax.axis_size(axis)
    return lax.ppermute(value, axis, [(i, i ^ distance) for i in range(length)])


def segment_sums(packed):
    length = lax.axis_size("seg")
    if length <= 4:
        return [packed] + [partners(packed, "seg", d) for d in range(1, length)]
    distance = 1
    while distance < length:
        packed = packed + partners(packed, "seg", distance)
        distance *= 2
    return [packed]


def after(value, *earlier):
    return lax.optimization_barrier((value, *earlier))


def on_device(voltages, filter_taps, positions, beam_dirs, chan_table):
    stations, width, snaps = voltages.shape
    channels = chan_table.shape[0]
    owners = lax.axis_size("stn")
    segments = lax.axis_size("seg")
    slots = channels // owners
    half = owners * stations
    snap_total = snaps * segments
    near, far = list(range(1, owners // 2)), list(range(owners // 2, owners))
    order = list(range(owners))
    late_ones = far[len(far) // 2 :]
    known = (owners - len(late_ones)) * stations
    split = far[:1] + near[1:] + far[1:2]
    rest = [d for d in order if d not in split]
    layout = [[(slot, d) for slot in range(slots)] for d in split + rest]
    halo = lax.ppermute(voltages[:, :, snaps - LANES :], "seg", [(i, i + 1) for i in range(segments - 1)])
    second = channelize(slots, "second", order, layout, chan_table, voltages, filter_taps)
    late = [partners(one, "stn", d) for d, one in zip(split, second)]
    joined = {key: (one, i) for keys, one in zip(layout[len(split) :], second[len(split) :]) for i, key in enumerate(keys)}
    *first, steer = channelize(
        slots, "first", order, layout, chan_table, voltages, filter_taps, halo, positions, beam_dirs, joined
    )
    at = len(split) - 1
    first, steer, late[:at] = after(first, steer, late[:at])
    first[at], late[at] = after(first[at], late[at])
    first = dict(zip(split + rest, first))
    arrived = {d: partners(first[d], "stn", d) for d in split + rest[1:] if d not in late_ones}
    following = {}
    for i, d in enumerate(late_ones):
        ahead = [far[i]] + (near[1:] if d == far[-1] else [])
        value, there = after(first[d], [arrived[e] for e in ahead])
        arrived.update(zip(ahead, there))
        following[d] = partners(value, "stn", d)
    arrived.update({0: first[0], **following})
    held = {(slot, d): [(one, slot)] for d, one in arrived.items() for slot in range(slots)}
    for d, one in zip(split, late):
        for slot in range(slots):
            held[slot, d].append((one, slot))
    blocks = lambda ds: [[held[slot, d] for d in ds] for slot in range(slots)]
    grams = segment_sums(first_gram(blocks([d for d in order if d not in late_ones]), known, half))
    swept = first_solve(snap_total, grams, steer)
    following, swept = after(following, swept)
    held.update({(slot, d): [(one, slot)] for d, one in following.items() for slot in range(slots)})
    grams = segment_sums(last_gram(blocks(order), len(late_ones), half - known, half))
    return beams(snap_total, grams, swept, steer, blocks(order))


def solution(mesh):
    return jax.shard_map(
        on_device,
        mesh=mesh,
        in_specs=(P("stn", None, "seg"), P(), P(), P(), P()),
        out_specs=P("stn", None, None, "seg"),
        check_vma=False,
    )
```

```python
import functools
import math

import jax
import jax.numpy as jnp
from jax import lax
from jax.experimental import pallas as pl
from jax.experimental.pallas import tpu as pltpu
from jax.sharding import PartitionSpec as P

DIRS = 360
LANES = 128
GROUP = 8
PIVOTS = 16
QUICK = pl.CostEstimate(flops=1000, bytes_accessed=1000, transcendentals=0)
AT_ONCE = 4
VMEM_BYTES = 16 << 20
GRAM_VMEM = 8 << 20
BEAMS_VMEM = 12 << 20

loading_level = 0.1
full_turn = 2.0 * math.pi
NN = (((1,), (0,)), ((), ()))
NT = (((1,), (1,)), ((), ()))
TN = (((0,), (0,)), ((), ()))
f32, bf16 = jnp.float32, jnp.bfloat16


def split_in_two(value):
    high = value.astype(bf16)
    return high, (value - high.astype(f32)).astype(bf16)


def merged_rows(pieces):
    if all(piece.shape[0] % 16 == 0 for piece in pieces):
        return jnp.concatenate(pieces, axis=0)
    return jnp.concatenate([piece.astype(f32) for piece in pieces], axis=0).astype(bf16)


def dft_rows(channels, width):
    shape = (2 * len(channels), GROUP * width)
    row = lax.broadcasted_iota(jnp.int32, shape, 0)
    lane = lax.broadcasted_iota(jnp.int32, shape, 1)
    channel = jnp.zeros(shape, jnp.int32)
    for index, one in enumerate(channels):
        channel = jnp.where(row // 2 == index, one, channel)
    angle = lax.rem(channel * lax.rem(lane, width), width).astype(f32) * (full_turn / width)
    values = jnp.where(row % 2 == 0, jnp.cos(angle), -jnp.sin(angle))
    shape = (GROUP, GROUP * width)
    own = lax.broadcasted_iota(jnp.int32, shape, 1) // width == lax.broadcasted_iota(jnp.int32, shape, 0)
    spread = [jnp.where(own, jnp.broadcast_to(values[i : i + 1], shape), 0.0) for i in range(2 * len(channels))]
    return jnp.concatenate(spread, axis=0)


def steering(me, order, positions, beam_dirs, channel, channels):
    owners = len(order)
    stations = positions.shape[1] // owners
    columns = jnp.concatenate([positions, jnp.zeros((6, positions.shape[1]), f32)], axis=0).T
    span = 1
    while span < owners:
        parts = [columns[i * stations : (i + 1) * stations] for i in range(owners)]
        turned = jnp.concatenate([parts[i ^ span] for i in range(owners)], axis=0)
        columns = jnp.where((me & span) != 0, turned, columns)
        span *= 2
    columns = jnp.concatenate([columns[d * stations : (d + 1) * stations] for d in order], axis=0)
    bearing = beam_dirs.astype(f32) * (full_turn / DIRS)
    frequency = 1.0 + channel.astype(f32) / channels
    path_delay = columns[:, 0:1] * jnp.cos(bearing) + columns[:, 1:2] * jnp.sin(bearing)
    turns = frequency * path_delay
    phases = full_turn * (turns - jnp.round(turns))
    return jnp.concatenate([jnp.cos(phases), jnp.sin(phases)], axis=0)


def channelize_kernel(owners, slots, part, order, places, joined, other_count, *refs):
    count = owners * slots
    has_halo = part != "second"
    chans_in, volts, taps_in = refs[:3]
    others = refs[3 + 3 * has_halo : 3 + 3 * has_halo + other_count]
    outs = refs[3 + 3 * has_halo + other_count : len(refs) - 10]
    dft, held, high, low, chans, taps, sems, chans_sem, taps_sem, halo_sem = refs[-10:]
    stations, width, snaps = volts.shape
    chunk = held.shape[2] - LANES
    tap_count = taps.shape[0]
    step = tap_count // 2
    rows = 2 * GROUP
    half = count * rows
    pieces = sems.shape[0]
    piece = stations // pieces
    small = [pltpu.make_async_copy(chans_in, chans, chans_sem), pltpu.make_async_copy(taps_in, taps, taps_sem)]
    if has_halo:
        small.append(pltpu.make_async_copy(refs[3], held.at[:, :, :LANES], halo_sem))
    copies = []
    for index in range(pieces):
        members = pl.ds(index * piece, piece)
        if has_halo:
            source, target = volts.at[members, :, :chunk], held.at[members, :, LANES:]
        else:
            source, target = volts.at[members, :, snaps - chunk - LANES :], held.at[members]
        copies.append(pltpu.make_async_copy(source, target, sems.at[index]))
    for copy in small + copies:
        copy.start()
    for copy in small:
        copy.wait()

    me = lax.axis_index("stn")
    table = dft_rows([chans[(me ^ d) * slots + slot] for slot in range(slots) for d in range(owners)], width)
    dft[:half], dft[half:] = split_in_two(table)
    columns = taps[...].T
    tap = [jnp.broadcast_to(columns[:, m : m + 1], (width, chunk + LANES)) for m in range(tap_count)]
    results = []
    for station in range(stations):
        if station % piece == 0:
            copies[station // piece].wait()
        now = held[station]
        shifted = [(pltpu.roll(now, m, axis=1) if m else now).astype(f32) for m in range(step)]
        near = sum(tap[m] * shifted[m] for m in range(step))
        far = sum(tap[step + m] * shifted[m] for m in range(step))
        filtered = (near + pltpu.roll(far, step, axis=1))[:, LANES:]
        member = station % GROUP
        high[pl.ds(member * width, width), :], low[pl.ds(member * width, width), :] = split_in_two(filtered)
        if member == GROUP - 1:
            both = jnp.dot(dft[...], high[...], preferred_element_type=f32)
            cross = jnp.dot(dft[:half], low[...], preferred_element_type=f32)
            results.append(both[:half] + (both[half:] + cross))
    for index in range(count):
        slot, d = divmod(index, owners)
        number, entry = places[slot, d]
        target = outs[number].at[entry]
        for real in range(2):
            first = index * rows + real * GROUP
            merged = jnp.concatenate([one[first : first + GROUP] for one in results], axis=0)
            target[real, :, :chunk] = merged.astype(bf16)
        if (slot, d) in joined:
            at, inside = joined[slot, d]
            target[:, :, chunk:] = others[at][inside]
    if has_halo:
        for slot in range(slots):
            channel = chans[me * slots + slot]
            outs[-1][slot] = steering(me, order, refs[4][...], refs[5][...], channel, owners * slots)


def channelize(slots, part, order, layout, chans, volts, taps, halo=None, positions=None, beam_dirs=None, joined=None):
    stations, width, snaps = volts.shape
    owners = len(order)
    count = owners * slots
    chunk = snaps // 2
    pieces = max(stations // 4, 1)
    joined = joined or {}
    others = []
    for array, _ in joined.values():
        if not any(array is one for one in others):
            others.append(array)
    number_of = lambda array: next(i for i, one in enumerate(others) if one is array)
    joined = {key: (number_of(array), entry) for key, (array, entry) in joined.items()}
    places, out_shape = {}, []
    for number, keys in enumerate(layout):
        for entry, key in enumerate(keys):
            places[key] = (number, entry)
        length = snaps if keys[0] in joined else chunk
        out_shape.append(jax.ShapeDtypeStruct((len(keys), 2, stations, length), bf16))
    if halo is not None:
        out_shape.append(jax.ShapeDtypeStruct((slots, 2 * owners * stations, beam_dirs.shape[0]), f32))
    operands = [pltpu.with_memory_space_constraint(one, pltpu.HBM) for one in (chans, volts, taps)]
    operands += ([] if halo is None else [halo, positions, beam_dirs[None, :]]) + others
    return pl.pallas_call(
        functools.partial(channelize_kernel, owners, slots, part, order, places, joined, len(others)),
        in_specs=[pl.BlockSpec(memory_space=pltpu.HBM)] * 3
        + [pl.BlockSpec(memory_space=pl.ANY)] * (halo is not None)
        + [pl.BlockSpec(memory_space=pltpu.VMEM)] * (len(operands) - 3 - (halo is not None)),
        out_specs=[pl.BlockSpec(memory_space=pltpu.VMEM)] * len(out_shape),
        out_shape=out_shape,
        scratch_shapes=[
            pltpu.VMEM((4 * count * GROUP, GROUP * width), bf16),
            pltpu.VMEM((stations, width, chunk + LANES), bf16),
            pltpu.VMEM((GROUP * width, chunk), bf16),
            pltpu.VMEM((GROUP * width, chunk), bf16),
            pltpu.SMEM(chans.shape, jnp.int32),
            pltpu.VMEM(taps.shape, f32),
            pltpu.SemaphoreType.DMA((pieces,)),
            pltpu.SemaphoreType.DMA(()),
            pltpu.SemaphoreType.DMA(()),
            pltpu.SemaphoreType.DMA(()),
        ],
        compiler_params=pltpu.CompilerParams(vmem_limit_bytes=VMEM_BYTES),
        cost_estimate=QUICK,
        name="channelize_" + part,
    )(*operands)


def flattened(blocks):
    arrays, numbered = [], []
    for block in blocks:
        numbered.append([])
        for array, entry in block:
            found = [i for i, one in enumerate(arrays) if one is array]
            if not found:
                found = [len(arrays)]
                arrays.append(array)
            numbered[-1].append((found[0], entry))
    return arrays, numbered


def stacked_rows(blocks, refs):
    rows = []
    for part in range(2):
        for block in blocks:
            rows.append(jnp.concatenate([refs[at][entry, part] for at, entry in block], axis=1))
    return merged_rows(rows)


def first_gram_kernel(blocks, *refs):
    out = refs[-1]
    slots, half, wide = out.shape
    row = lax.broadcasted_iota(jnp.int32, (half, half), 0)
    column = lax.broadcasted_iota(jnp.int32, (half, half), 1)
    for slot in range(slots):
        stacked = stacked_rows(blocks[slot], refs[:-1])
        gram = lax.dot_general(stacked, stacked, NT, preferred_element_type=f32)
        sym_part = gram[:half, :half] + gram[half:, half:]
        skew_part = gram[half:, :half] - gram[:half, half:]
        packed = jnp.where(row >= column, sym_part, skew_part)
        out[slot] = jnp.concatenate([packed, jnp.zeros((half, wide - half), f32)], axis=1)


def last_gram_kernel(blocks, count, *refs):
    out = refs[-1]
    slots, double, half = out.shape
    rows = double // 2
    for slot in range(slots):
        stacked = stacked_rows(blocks[slot], refs[:-1])
        ours = stacked_rows(blocks[slot][-count:], refs[:-1])
        gram = lax.dot_general(ours, stacked, NT, preferred_element_type=f32)
        out[slot, :rows] = gram[:rows, :half] + gram[rows:, half:]
        out[slot, rows:] = gram[rows:, :half] - gram[:rows, half:]


def gram_call(kernel, blocks, shape, name):
    operands, numbered = flattened([block for one in blocks for block in one])
    per_slot = len(blocks[0])
    numbered = [numbered[i * per_slot : (i + 1) * per_slot] for i in range(len(blocks))]
    return pl.pallas_call(
        functools.partial(kernel, numbered),
        in_specs=[pl.BlockSpec(memory_space=pltpu.VMEM)] * len(operands),
        out_specs=pl.BlockSpec(memory_space=pltpu.VMEM),
        out_shape=jax.ShapeDtypeStruct((len(blocks), *shape), f32),
        compiler_params=pltpu.CompilerParams(vmem_limit_bytes=GRAM_VMEM),
        cost_estimate=QUICK,
        name=name,
    )(*operands)


def first_gram(blocks, stations, half):
    return gram_call(first_gram_kernel, blocks, (stations, half), "first_gram")


def last_gram(blocks, count, stations, half):
    kernel = lambda numbered, *refs: last_gram_kernel(numbered, count, *refs)
    return gram_call(kernel, blocks, (2 * stations, half), "last_gram")


def dot(left, right, dims=NN):
    return lax.dot_general(left, right, dims, precision=lax.Precision.HIGHEST, preferred_element_type=f32)


def split_in_three(value):
    high, rest = value.astype(bf16), value
    rest = rest - high.astype(f32)
    middle = rest.astype(bf16)
    return high, middle, (rest - middle.astype(f32)).astype(bf16)


def deep_dot(left, right):
    a, b = split_in_three(left), split_in_three(right)
    left = jnp.concatenate([a[0], a[0], a[1], a[1], a[0], a[2]], axis=0)
    right = jnp.concatenate([b[0], b[1], b[0], b[1], b[2], b[0]], axis=0)
    return lax.dot_general(left, right, TN, preferred_element_type=f32)


def sweep_rows(systems, lanes, at_once):
    count, width = systems[0][0].shape
    narrow = (count, LANES)
    index, index_wide = (lax.broadcasted_iota(jnp.int32, shape, 0) for shape in (narrow, (count, width)))
    repeated = lambda value: jnp.concatenate([value] * (width // LANES), axis=1)
    rows = list(systems)
    for start in range(0, count, at_once):
        fetched = lanes[start : start + at_once]
        columns = [
            [tuple(jnp.broadcast_to(part[:, lane : lane + 1], narrow) for part in row) for lane in fetched] for row in rows
        ]
        for j in range(len(fetched)):
            step = start + j
            spread = lambda value: jnp.broadcast_to(value[step : step + 1], value.shape)

            def swept(value, here, a, b, scale):
                real, imag = value
                pick_r, pick_i = spread(real) * scale, spread(imag) * scale
                return (
                    jnp.where(here, pick_r, real - (a * pick_r - b * pick_i)),
                    jnp.where(here, pick_i, imag - (a * pick_i + b * pick_r)),
                )

            scales = [1.0 / spread(column[j][0]) for column in columns]
            for later in range(j + 1, len(fetched)):
                for column, scale in zip(columns, scales):
                    column[later] = swept(column[later], index == step, *column[j], scale)
            for number, (column, scale) in enumerate(zip(columns, scales)):
                a, b = column[j]
                rows[number] = swept(rows[number], index_wide == step, repeated(a), repeated(b), repeated(scale))
    return rows


def eliminate(systems, start, stop, pivots, at_once):
    half = systems[0][0].shape[0]
    shape = systems[0][0].shape
    rank = lax.broadcasted_iota(jnp.int32, shape, 0)
    lane = lax.broadcasted_iota(jnp.int32, shape, 1)
    for first in range(start, stop, pivots):
        last = first + pivots
        tile = first // LANES * LANES
        inside = (lane[first:last] >= first) & (lane[first:last] < last)
        minus_one = jnp.where(rank[first:last] == lane[first:last], -1.0, 0.0)
        sides, rows = [], []
        for real, imag in systems:
            row_r, row_i = real[first:last], imag[first:last]
            upper = jnp.concatenate([row_r[:, :half], -row_i[:, :half]], axis=1)
            lower = jnp.concatenate([row_i[:, :half], row_r[:, :half]], axis=1)
            sides.append(jnp.concatenate([upper, lower], axis=0))
            rows.append((
                jnp.concatenate([row_r[:, tile : tile + LANES], jnp.where(inside, minus_one, row_r)], axis=1),
                jnp.concatenate([row_i[:, tile : tile + LANES], jnp.where(inside, 0.0, row_i)], axis=1),
            ))
        rows = sweep_rows(rows, range(first - tile, last - tile), at_once)
        own = (rank >= first) & (rank < last)
        gone = (lane >= first) & (lane < last)
        spread = lambda piece: jnp.concatenate([piece] * (half // pivots), axis=0)
        results = []
        for (real, imag), side, (row_r, row_i) in zip(systems, sides, rows):
            row_r, row_i = row_r[:, LANES:], row_i[:, LANES:]
            update = deep_dot(side, jnp.concatenate([row_r, row_i], axis=0))
            results.append((
                jnp.where(own, spread(row_r), jnp.where(gone, 0.0, real) - update[:half]),
                jnp.where(own, spread(row_i), jnp.where(gone, 0.0, imag) - update[half:]),
            ))
        systems = results
    return systems


def first_solve_kernel(segments, snap_total, *refs):
    grams, steer, out = refs[:segments], refs[segments], refs[-1]
    slots, stations, half = grams[0].shape
    row = lax.broadcasted_iota(jnp.int32, (half, half), 0)
    column = lax.broadcasted_iota(jnp.int32, (half, half), 1)
    systems = []
    for slot in range(slots):
        packed = sum(one[slot] for one in grams) * (1.0 / snap_total)
        if stations < half:
            packed = jnp.concatenate([packed, jnp.zeros((half - stations, half), f32)], axis=0)
        turned = packed.T
        real = jnp.where(row >= column, packed, turned)
        real = jnp.where((row == column) & (row < stations), real + loading_level, real)
        imag = jnp.where(row < column, packed, jnp.where(row > column, -turned, 0.0))
        known = row < stations
        systems.append((
            jnp.concatenate([real, jnp.where(known, steer[slot, :half], 0.0)], axis=1),
            jnp.concatenate([imag, jnp.where(known, steer[slot, half:], 0.0)], axis=1),
        ))
    for slot, (real, imag) in enumerate(eliminate(systems, 0, stations, math.gcd(stations, PIVOTS), AT_ONCE)):
        out[slot, 0] = jnp.concatenate([real, systems[slot][0][:, :half]], axis=1)
        out[slot, 1] = jnp.concatenate([imag, systems[slot][1][:, :half]], axis=1)


def first_solve(snap_total, grams, steer):
    slots, _, count = steer.shape
    half = grams[0].shape[2]
    return pl.pallas_call(
        functools.partial(first_solve_kernel, len(grams), snap_total),
        in_specs=[pl.BlockSpec(memory_space=pltpu.VMEM)] * (len(grams) + 1),
        out_specs=pl.BlockSpec(memory_space=pltpu.VMEM),
        out_shape=jax.ShapeDtypeStruct((slots, 2, half, 2 * half + count), f32),
        compiler_params=pltpu.CompilerParams(vmem_limit_bytes=BEAMS_VMEM),
        cost_estimate=QUICK,
        name="first_solve",
    )(*grams, steer)


def complex_rows(real, imag):
    upper = jnp.concatenate([real, -imag], axis=1)
    return jnp.concatenate([upper, jnp.concatenate([imag, real], axis=1)], axis=0)


def joined_system(swept_r, swept_i, rows_r, rows_i, steer_r, steer_i, known):
    count, half = rows_r.shape
    end = half + steer_r.shape[1]
    lane = lax.broadcasted_iota(jnp.int32, rows_r.shape, 1)
    cross_r, cross_i = jnp.where(lane < known, rows_r, 0.0), jnp.where(lane < known, rows_i, 0.0)
    stacked = lambda first, last: jnp.concatenate([swept_r[:, first:last], swept_i[:, first:last]], axis=0)
    inverse, matrix = stacked(0, half), stacked(end, end + half)
    guess = -dot(complex_rows(cross_r, cross_i), inverse)
    rest = jnp.concatenate([cross_r, cross_i], axis=0) - dot(complex_rows(guess[:count], guess[count:]), matrix)
    guess = guess - dot(complex_rows(rest[:count], rest[count:]), inverse)
    turn_r, turn_i = guess[:count], guess[count:]
    ahead = lax.broadcasted_iota(jnp.int32, steer_r.shape, 0) < known
    first_steer = jnp.concatenate([jnp.where(ahead, steer_r, 0.0), jnp.where(ahead, steer_i, 0.0)], axis=0)
    taken = dot(complex_rows(turn_r, turn_i), first_steer)
    back_r, back_i = steer_r[known:] - taken[:count], steer_i[known:] - taken[count:]
    left = jnp.concatenate(
        [jnp.concatenate([turn_r, turn_i], axis=1), jnp.concatenate([turn_i, -turn_r], axis=1)], axis=0
    )
    right = jnp.concatenate([jnp.zeros((known, 2 * half), f32), jnp.concatenate([cross_r, cross_i], axis=1)], axis=0)
    inner = dot(left, right, NT)
    rows_r = jnp.where(lane < known, turn_r, rows_r - inner[:count])
    rows_i = jnp.where(lane < known, turn_i, rows_i - inner[count:])
    real = jnp.concatenate([swept_r[:known, :end], jnp.concatenate([rows_r, back_r], axis=1)], axis=0)
    imag = jnp.concatenate([swept_i[:known, :end], jnp.concatenate([rows_i, back_i], axis=1)], axis=0)
    return real, imag


def beams_kernel(segments, snap_total, blocks, *refs):
    grams, swept, steer = refs[:segments], refs[segments], refs[segments + 1]
    arrays, (out, mix, mixed_beams, sems) = refs[segments + 2 : -4], refs[-4:]
    slots, double, half = grams[0].shape
    known = half - double // 2
    count = steer.shape[2]

    systems = []
    shape = (double // 2, half)
    diagonal = lax.broadcasted_iota(jnp.int32, shape, 0) + known == lax.broadcasted_iota(jnp.int32, shape, 1)
    for slot in range(slots):
        rows = sum(one[slot] for one in grams) * (1.0 / snap_total)
        rows_r, rows_i = rows[: double // 2], rows[double // 2 :]
        rows_r = jnp.where(diagonal, rows_r + loading_level, rows_r)
        steer_r, steer_i = steer[slot, :half], steer[slot, half:]
        systems.append(joined_system(swept[slot, 0], swept[slot, 1], rows_r, rows_i, steer_r, steer_i, known))
    for slot, (real, imag) in enumerate(eliminate(systems, known, half, math.gcd(known, PIVOTS), AT_ONCE)):
        solved_r, solved_i = real[:, half:], imag[:, half:]
        power = jnp.sum(steer[slot, :half] * solved_r + steer[slot, half:] * solved_i, axis=0, keepdims=True)
        scale = 1.0 / jnp.sqrt(power)
        weight_r, weight_i = (solved_r * scale).T, (solved_i * scale).T
        mix[slot, :count] = jnp.concatenate([weight_r, weight_i], axis=1).astype(bf16)
        mix[slot, count:] = jnp.concatenate([-weight_i, weight_r], axis=1).astype(bf16)

    copies = []
    for slot in range(slots):
        stacked = stacked_rows(blocks[slot], arrays)
        for part in range(2):
            rows = mix[slot, part * count : (part + 1) * count]
            mixed_beams[slot, part] = jnp.dot(rows, stacked, preferred_element_type=f32).astype(bf16)
            copies.append(pltpu.make_async_copy(mixed_beams.at[slot, part], out.at[slot, part], sems.at[slot, part]))
            copies[-1].start()
    for copy in copies:
        copy.wait()


def beams(snap_total, grams, swept, steer, blocks):
    slots, double, count = steer.shape
    arrays, numbered = flattened([block for one in blocks for block in one])
    per_slot = len(blocks[0])
    numbered = [numbered[i * per_slot : (i + 1) * per_slot] for i in range(slots)]
    snaps = sum(array.shape[-1] for array, _ in blocks[0][0])
    operands = [*grams, swept, steer, *arrays]
    return pl.pallas_call(
        functools.partial(beams_kernel, len(grams), snap_total, numbered),
        in_specs=[pl.BlockSpec(memory_space=pltpu.VMEM)] * len(operands),
        out_specs=pl.BlockSpec(memory_space=pltpu.HBM),
        out_shape=jax.ShapeDtypeStruct((slots, 2, count, snaps), bf16),
        scratch_shapes=[
            pltpu.VMEM((slots, 2 * count, double), bf16),
            pltpu.VMEM((slots, 2, count, snaps), bf16),
            pltpu.SemaphoreType.DMA((slots, 2)),
        ],
        compiler_params=pltpu.CompilerParams(vmem_limit_bytes=BEAMS_VMEM),
        cost_estimate=QUICK,
        name="beams",
    )(*operands)


def partners(value, axis, distance):
    length = lax.axis_size(axis)
    return lax.ppermute(value, axis, [(i, i ^ distance) for i in range(length)])


def segment_sums(packed):
    length = lax.axis_size("seg")
    if length <= 4:
        return [packed] + [partners(packed, "seg", d) for d in range(1, length)]
    distance = 1
    while distance < length:
        packed = packed + partners(packed, "seg", distance)
        distance *= 2
    return [packed]


def after(value, *earlier):
    return lax.optimization_barrier((value, *earlier))


def on_device(voltages, filter_taps, positions, beam_dirs, chan_table):
    stations, width, snaps = voltages.shape
    channels = chan_table.shape[0]
    owners = lax.axis_size("stn")
    segments = lax.axis_size("seg")
    slots = channels // owners
    half = owners * stations
    snap_total = snaps * segments
    near, far = list(range(1, owners // 2)), list(range(owners // 2, owners))
    order = list(range(owners))
    late_ones = far[len(far) // 2 :]
    known = (owners - len(late_ones)) * stations
    split = far[:1] + near[1:] + far[1:2]
    rest = [d for d in order if d not in split]
    layout = [[(slot, d) for slot in range(slots)] for d in split + rest]
    halo = lax.ppermute(voltages[:, :, snaps - LANES :], "seg", [(i, i + 1) for i in range(segments - 1)])
    second = channelize(slots, "second", order, layout, chan_table, voltages, filter_taps)
    late = [partners(one, "stn", d) for d, one in zip(split, second)]
    joined = {key: (one, i) for keys, one in zip(layout[len(split) :], second[len(split) :]) for i, key in enumerate(keys)}
    *first, steer = channelize(
        slots, "first", order, layout, chan_table, voltages, filter_taps, halo, positions, beam_dirs, joined
    )
    first, steer, late = after(first, steer, late)
    first = dict(zip(split + rest, first))
    arrived = {d: partners(first[d], "stn", d) for d in split + rest[1:] if d not in late_ones}
    following = {}
    for i, d in enumerate(late_ones):
        ahead = [far[i]] + (near[1:] if d == far[-1] else [])
        value, there = after(first[d], [arrived[e] for e in ahead])
        arrived.update(zip(ahead, there))
        following[d] = partners(value, "stn", d)
    arrived.update({0: first[0], **following})
    held = {(slot, d): [(one, slot)] for d, one in arrived.items() for slot in range(slots)}
    for d, one in zip(split, late):
        for slot in range(slots):
            held[slot, d].append((one, slot))
    blocks = lambda ds: [[held[slot, d] for d in ds] for slot in range(slots)]
    grams = segment_sums(first_gram(blocks([d for d in order if d not in late_ones]), known, half))
    swept = first_solve(snap_total, grams, steer)
    following, swept = after(following, swept)
    held.update({(slot, d): [(one, slot)] for d, one in following.items() for slot in range(slots)})
    grams = segment_sums(last_gram(blocks(order), len(late_ones), half - known, half))
    return beams(snap_total, grams, swept, steer, blocks(order))


def solution(mesh):
    return jax.shard_map(
        on_device,
        mesh=mesh,
        in_specs=(P("stn", None, "seg"), P(), P(), P(), P()),
        out_specs=P("stn", None, None, "seg"),
        check_vma=False,
    )
```
